32 devices in a mesh: tgt: 8 (over z, core), src: 4 (over y, x).
Axes of the slice: x: 2, y: 2, z: 4, core: 2. Of those that a mesh axis runs over, the one named last changes fastest.
Arguments:
- tgt_weight: bfloat16 [256, 16, 4096], P('tgt', 'src'), may hold values from -0.75 to 0.75
- src_weight: bfloat16 [128, 16, 4096], P('src', 'tgt'), may hold values from -0.75 to 0.75
- coupling: bfloat16 [24576, 4096], P(('tgt', 'src')), may hold values from -6 to 6
- block_tgt: int32 [24576], P(('tgt', 'src')), may hold values from 0 to 255, as said below
- block_src: int32 [24576], P(('tgt', 'src')), may hold values from 0 to 127, as said below
- block_cone: int32 [24576], P(('tgt', 'src')), may hold values from 0 to 15
- block_count: int32 [32], P(('tgt', 'src')), may hold values from 1 to 768, as said below
- tgt_transfer: bfloat16 [256, 16, 4096], P('tgt', 'src'), may hold values from -0.75 to 0.75
Outputs:
- new_coupling: bfloat16 [24576, 4096], P(('tgt', 'src'))
- new_transfer: bfloat16 [256, 16, 4096], P('tgt', 'src')
The draws below stay inside these ranges and needn't reach their ends.
Inputs may be any that keep to these rules, and one draw needn't show every extreme that they name: `block_tgt`: A slot on the device with tgt index i and src index j names a target cluster of i * 32 to (i + 1) * 32 - 1. `block_src`: A slot on the device with tgt index i and src index j names a source cluster of j * 32 to (j + 1) * 32 - 1. Device d's live slots are its first block_count[d]; some device is full.
All inputs are finite; a program needn't handle non-finite values.
Results may differ from the reference program's by a relative error of at most 0.0051.
Values may be sent and summed in bfloat16 or wider, within the bound.
No kernel may reach another device: no remote copies, remote signals or barrier semaphores. Data moves between devices by JAX's collectives and lax.ppermute only.
A program may use at most 192 MiB of HBM per device.

```python
import jax
import jax.numpy as jnp
from jax import lax

W = 64
WW = 4096
CONES = 16
CT_DEV = 32
CS_DEV = 32
BLK_DEV = 768
TGT_CLU = 256
SRC_CLU = 128
NDEV = 32
BLOCKS = 24576
N_SRC = 4


def draw_block_tgt(key, part):
    key = jax.random.fold_in(key, 11)
    device = jnp.arange(BLOCKS, dtype=jnp.int32) // BLK_DEV
    rowidx = device // N_SRC
    return rowidx * CT_DEV + jax.random.randint(key, (BLOCKS,), 0, CT_DEV, dtype=jnp.int32)


def draw_block_src(key, part):
    key = jax.random.fold_in(key, 23)
    device = jnp.arange(BLOCKS, dtype=jnp.int32) // BLK_DEV
    colidx = device % N_SRC
    return colidx * CS_DEV + jax.random.randint(key, (BLOCKS,), 0, CS_DEV, dtype=jnp.int32)


def draw_block_count(key, part):
    key = jax.random.fold_in(key, 37)
    first, second = jax.random.split(key)
    counts = jax.random.randint(first, (NDEV,), BLK_DEV // 4, BLK_DEV + 1, dtype=jnp.int32)
    full = jax.random.randint(second, (), 0, NDEV, dtype=jnp.int32)
    return jnp.where(jnp.arange(NDEV, dtype=jnp.int32) == full, BLK_DEV, counts)


def plant(drawn, stream_key, low, top_value):
    place = [jax.random.randint(jax.random.fold_in(stream_key, axis), (), 0, length) for axis, length in enumerate(drawn.shape)]
    widest = drawn.shape.index(max(drawn.shape))
    beside = place[:widest] + [(place[widest] + 1) % drawn.shape[widest]] + place[widest + 1:]
    return drawn.at[tuple(place)].set(low).at[tuple(beside)].set(top_value)


def levels(own_key, dims, cuts, low, largest):
    level = 1.0
    for axis_at, parts in cuts:
        steps = jax.random.uniform(jax.random.fold_in(jax.random.fold_in(own_key, 6), axis_at), (parts,), jnp.float32, low / len(cuts), largest / len(cuts))
        level = level * jnp.repeat(jnp.exp(steps), dims[axis_at] // parts).reshape((-1,) + (1,) * (len(dims) - 1 - axis_at))
    return level


def scatter_about(stream_key, extent, spread, bound, cuts=(), kind=jnp.bfloat16):
    array = spread * jax.random.normal(stream_key, extent, jnp.float32)
    if cuts:
        array = array * levels(stream_key, extent, cuts, -0.22, 0.18)
    return jnp.clip(array, -bound, bound).astype(kind)


def setup_inputs(seed: int = 0) -> dict:
    splits = jax.random.split(jax.random.key(seed), 9)
    tgt_weight = scatter_about(splits[0], (TGT_CLU, CONES, WW), W ** -0.5, 0.75, ((0, 8), (1, 4)))
    src_weight = scatter_about(splits[1], (SRC_CLU, CONES, WW), W ** -0.5, 0.75, ((0, 4), (1, 8)))
    coupling = scatter_about(splits[2], (BLOCKS, WW), 1.0, 6.0, ((0, 32),))
    block_tgt = draw_block_tgt(jax.random.fold_in(splits[8], 71), 0)
    block_src = draw_block_src(jax.random.fold_in(splits[8], 71), 0)
    block_cone = plant(jax.random.randint(splits[5], (BLOCKS,), 0, CONES), jax.random.fold_in(splits[5], 1), 0, CONES - 1).astype(jnp.int32)
    block_count = draw_block_count(jax.random.fold_in(splits[8], 71), 0)
    tgt_transfer = scatter_about(splits[7], (TGT_CLU, CONES, WW), W ** -0.5, 0.75, ((0, 8), (1, 4)))
    return dict(tgt_weight=tgt_weight, src_weight=src_weight, coupling=coupling, block_tgt=block_tgt, block_src=block_src, block_cone=block_cone, block_count=block_count, tgt_transfer=tgt_transfer)


def reference(tgt_weight, src_weight, coupling, block_tgt, block_src, block_cone, block_count, tgt_transfer):
    tflat = tgt_weight.reshape(TGT_CLU * CONES, W, W)
    sflat = src_weight.reshape(SRC_CLU * CONES, W, W)

    def one_device(packed):
        rows, tids, sids, cids, count = packed
        twt = tflat[tids * CONES + cids].astype(jnp.float32)
        swt = sflat[sids * CONES + cids].astype(jnp.float32)
        blocks = rows.reshape(-1, W, W).astype(jnp.float32)
        left = jnp.einsum('bij,bjk->bik', twt, blocks).astype(jnp.bfloat16)
        outer = jnp.einsum('bij,bkj->bik', left.astype(jnp.float32), swt)
        keep = jnp.arange(BLK_DEV, dtype=jnp.int32) < count
        return jnp.where(keep[:, None], outer.reshape(-1, WW), 0.0).astype(jnp.bfloat16)

    packed = (coupling.reshape(NDEV, BLK_DEV, WW), block_tgt.reshape(NDEV, BLK_DEV),
              block_src.reshape(NDEV, BLK_DEV), block_cone.reshape(NDEV, BLK_DEV), block_count)
    new_coupling = lax.map(one_device, packed).reshape(BLOCKS, WW)
    transfer = jnp.einsum('bij,bjk->bik', tflat.astype(jnp.float32),
                          tgt_transfer.reshape(-1, W, W).astype(jnp.float32))
    new_transfer = transfer.reshape(TGT_CLU, CONES, WW).astype(jnp.bfloat16)
    return new_coupling, new_transfer
```

```python
import functools

import jax
import jax.numpy as jnp
from jax import lax
from jax.experimental import pallas as pl
from jax.experimental.pallas import tpu as pltpu
from jax.sharding import PartitionSpec as P

W = 64
WW = 4096
CONES = 16
H = W // 2
LANES = 2 * W
CHUNKS = WW // LANES
PITCH = H + 1
GROUP = 16
f32, bf16 = jnp.float32, jnp.bfloat16
VMEM_LIMIT = 60 * 2**20


def swap_halves(x):
    return jnp.concatenate([x[:, W:], x[:, :W]], axis=1)


def low_lanes():
    return lax.broadcasted_iota(jnp.int32, (H, LANES), 1) < W


def left_product(t, c, low):
    lhs = jnp.concatenate([t[:, :W], t[:, W:]], axis=0)
    rhs = jnp.concatenate([c, swap_halves(c)], axis=0)
    y = jnp.dot(lhs, rhs, preferred_element_type=f32)
    return jnp.where(low, y[:H], y[H:])


def right_product(left, s, low):
    lhs = jnp.concatenate([left[:, :W], left[:, W:]], axis=0).astype(bf16)
    turned = swap_halves(s)
    rhs = jnp.concatenate([jnp.where(low, s, turned), jnp.where(low, turned, s)], axis=0)
    y = jnp.dot(lhs, rhs, preferred_element_type=f32)
    return jnp.where(low, y[:H], y[H:])


def prep_kernel(t_ref, s_ref, t_out, s_out, t_scr, s_scr):
    def spread(ref, scr):
        cones = ref.shape[1]

        def one(i, carry):
            for c in range(CHUNKS):
                x = ref[i, :, c * LANES:(c + 1) * LANES].astype(f32)
                if cones == 1:
                    scr[pl.ds(i * PITCH + c, 1), :] = x
                else:
                    scr[pl.ds(i * (cones * PITCH) + c, cones, stride=PITCH), :] = x
            return carry

        lax.fori_loop(0, ref.shape[0], one, 0, unroll=2)

    spread(s_ref, s_scr)
    row = lax.broadcasted_iota(jnp.int32, (LANES, 4 * LANES), 0)
    lane = lax.broadcasted_iota(jnp.int32, (LANES, 4 * LANES), 1)
    same = (row // H) == (lane // LANES)
    even = jnp.where(same & (lane % W == 2 * (row % H)), 1.0, 0.0).astype(bf16)
    odd = jnp.where(same & (lane % W == 2 * (row % H) + 1), 1.0, 0.0).astype(bf16)
    low = low_lanes()

    def turn(i, carry):
        base = pl.multiple_of(i * (8 * PITCH), 8)
        part = s_scr.at[pl.ds(base, 8 * PITCH)]
        for half in range(2):
            four = jnp.concatenate(
                [part[m * PITCH:m * PITCH + H, :] for m in range(4 * half, 4 * half + 4)], axis=0
            )
            up = four.T.astype(bf16)
            both = jnp.dot(up[:W], even, preferred_element_type=f32) + jnp.dot(
                up[W:], odd, preferred_element_type=f32
            )
            for m in range(4):
                d = both[:, m * LANES:(m + 1) * LANES]
                s_out[i * 8 + 4 * half + m] = jnp.where(low, d[:H], d[H:]).astype(bf16)
        return carry

    lax.fori_loop(0, s_out.shape[0] // 8, turn, 0, unroll=2)

    spread(t_ref, t_scr)
    row = lax.broadcasted_iota(jnp.int32, (LANES, LANES), 0)
    lane = lax.broadcasted_iota(jnp.int32, (LANES, LANES), 1)
    g, at = lane // W, lane % W
    odd_col = (at // H) ^ g
    order = jnp.where(row == g * W + 2 * (at % H) + odd_col, 1.0, 0.0).astype(bf16)

    def sort(i, carry):
        base = pl.multiple_of(i * (8 * PITCH), 8)
        part = t_scr.at[pl.ds(base, 8 * PITCH)]
        eight = jnp.concatenate([part[m * PITCH:m * PITCH + H, :] for m in range(8)], axis=0)
        y = jnp.dot(eight.astype(bf16), order, preferred_element_type=f32).astype(bf16)
        for m in range(8):
            t_out[i * 8 + m] = y[m * H:(m + 1) * H]
        return carry

    lax.fori_loop(0, t_out.shape[0] // 8, sort, 0, unroll=2)


def prep(tgt_weight, src_weight):
    nt = tgt_weight.shape[0] * tgt_weight.shape[1]
    ns = src_weight.shape[0] * src_weight.shape[1]
    whole = pl.BlockSpec(memory_space=pltpu.VMEM)
    return pl.pallas_call(
        prep_kernel,
        in_specs=[whole, whole],
        out_specs=[whole, whole],
        out_shape=[
            jax.ShapeDtypeStruct((nt, H, LANES), bf16),
            jax.ShapeDtypeStruct((ns, H, LANES), bf16),
        ],
        scratch_shapes=[pltpu.VMEM((nt * PITCH, LANES), f32), pltpu.VMEM((ns * PITCH, LANES), f32)],
        compiler_params=pltpu.CompilerParams(vmem_limit_bytes=VMEM_LIMIT),
    )(tgt_weight, src_weight)


def transfer_kernel(t_ref, x_ref, o_ref, x_scr, o_scr):
    low = low_lanes()
    clusters, cones = x_ref.shape[0], x_ref.shape[1]
    per = max(1, 8 // cones)

    def one(i, carry):
        for u in range(per):
            for c in range(CHUNKS):
                x = x_ref[i * per + u, :, c * LANES:(c + 1) * LANES].astype(f32)
                if cones == 1:
                    x_scr[pl.ds(u * PITCH + c, 1), :] = x
                else:
                    x_scr[pl.ds(u * cones * PITCH + c, cones, stride=PITCH), :] = x
        for m in range(per * cones):
            x = x_scr[m * PITCH:m * PITCH + H, :].astype(bf16)
            y = left_product(t_ref[i * (per * cones) + m], x, low)
            o_scr[m * PITCH:m * PITCH + H, :] = y
        for u in range(per):
            for c in range(CHUNKS):
                if cones == 1:
                    y = o_scr[pl.ds(u * PITCH + c, 1), :]
                else:
                    y = o_scr[pl.ds(u * cones * PITCH + c, cones, stride=PITCH), :]
                o_ref[i * per + u, :, c * LANES:(c + 1) * LANES] = y.astype(bf16)
        return carry

    lax.fori_loop(0, clusters // per, one, 0, unroll=2)


def transfer(t_dense, tgt_transfer):
    whole = pl.BlockSpec(memory_space=pltpu.VMEM)
    cones = tgt_transfer.shape[1]
    rows = max(8, cones) * PITCH
    return pl.pallas_call(
        transfer_kernel,
        in_specs=[whole, whole],
        out_specs=whole,
        out_shape=jax.ShapeDtypeStruct(tgt_transfer.shape, bf16),
        scratch_shapes=[pltpu.VMEM((rows, LANES), f32)] * 2,
        compiler_params=pltpu.CompilerParams(vmem_limit_bytes=VMEM_LIMIT),
    )(t_dense, tgt_transfer)


def main_kernel(n_t, n_s, block, tid, sid, live, c_ref, *refs):
    t_parts, s_parts = refs[:n_t], refs[n_t:n_t + n_s]
    o_ref, t_tab, s_tab, c_scr, o_scr, sem = refs[n_t + n_s:]
    first = pl.program_id(0) * block
    low = low_lanes()

    @pl.when(pl.program_id(0) == 0)
    def _():
        copies = []
        for parts, tab in ((t_parts, t_tab), (s_parts, s_tab)):
            at = 0
            for part in parts:
                copies.append(
                    pltpu.make_async_copy(part, tab.at[pl.ds(at, part.shape[0])], sem.at[len(copies)])
                )
                at += part.shape[0]
        for copy in copies:
            copy.start()
        for copy in copies:
            copy.wait()

    def step(i, carry):
        i0 = pl.multiple_of(i * GROUP, GROUP)
        n0 = first + i0
        for c in range(CHUNKS):
            c_scr[pl.ds(c, GROUP, stride=PITCH), :] = c_ref[
                pl.ds(i0, GROUP), c * LANES:(c + 1) * LANES
            ].astype(f32)
        for n in range(GROUP):
            c = c_scr[n * PITCH:n * PITCH + H, :].astype(bf16)
            left = left_product(t_tab[tid[n0 + n]], c, low)
            o_scr[n * PITCH:n * PITCH + H, :] = right_product(left, s_tab[sid[n0 + n]], low)
        keep = lax.broadcasted_iota(jnp.int32, (GROUP, LANES), 0) + n0 < live[0]
        for c in range(CHUNKS):
            o = o_scr[pl.ds(c, GROUP, stride=PITCH), :]
            o_ref[pl.ds(i0, GROUP), c * LANES:(c + 1) * LANES] = jnp.where(keep, o, 0.0).astype(bf16)
        return carry

    @pl.when(first < live[0])
    def _():
        lax.fori_loop(0, block // GROUP, step, 0, unroll=4)

    @pl.when(first >= live[0])
    def _():
        o_ref[...] = jnp.zeros(o_ref.shape, bf16)


def main(coupling, tid, sid, live, t_parts, s_parts):
    slots = coupling.shape[0]
    block = 128
    n_t = sum(p.shape[0] for p in t_parts)
    n_s = sum(p.shape[0] for p in s_parts)
    anywhere = pl.BlockSpec(memory_space=pl.ANY)
    return pl.pallas_call(
        functools.partial(main_kernel, len(t_parts), len(s_parts), block),
        grid_spec=pltpu.PrefetchScalarGridSpec(
            num_scalar_prefetch=3,
            grid=(slots // block,),
            in_specs=[pl.BlockSpec((block, WW), lambda g, *_: (g, 0))]
            + [anywhere] * (len(t_parts) + len(s_parts)),
            out_specs=pl.BlockSpec((block, WW), lambda g, *_: (g, 0)),
            scratch_shapes=[
                pltpu.VMEM((n_t, H, LANES), bf16),
                pltpu.VMEM((n_s, H, LANES), bf16),
                pltpu.VMEM((GROUP * PITCH, LANES), f32),
                pltpu.VMEM((GROUP * PITCH, LANES), f32),
                pltpu.SemaphoreType.DMA((len(t_parts) + len(s_parts),)),
            ],
        ),
        out_shape=jax.ShapeDtypeStruct((slots, WW), bf16),
        compiler_params=pltpu.CompilerParams(vmem_limit_bytes=VMEM_LIMIT),
    )(tid, sid, live, coupling, *t_parts, *s_parts)


def gather_row(t_dense, n_src):
    if n_src != 4:
        every = lax.all_gather(t_dense, "src", axis=0, tiled=True)
        return [every], False
    x_pairs = [(i, i ^ 1) for i in range(4)]
    y_pairs = [(i, i ^ 2) for i in range(4)]
    half = t_dense.shape[0] // 2
    x = lax.ppermute(t_dense, "src", x_pairs)
    y = lax.ppermute(t_dense, "src", y_pairs)
    d0 = lax.ppermute(x[:half], "src", y_pairs)
    d1 = lax.ppermute(y[half:], "src", x_pairs)
    return [t_dense, x, y, d0, d1], True


def gather_column(s_dense, chips):
    def near(z):
        return z ^ 1

    def far(z):
        return z if z in (0, chips - 1) else ((z - 1) ^ 1) + 1

    a_pairs = [(2 * z + c, 2 * near(z) + c) for z in range(chips) for c in range(2)]
    b_pairs = [(2 * z + c, 2 * far(z) + c) for z in range(chips) for c in range(2)]
    cores = [(i, i ^ 1) for i in range(2 * chips)]
    a, b = s_dense, s_dense
    a_side, b_side = [], []
    for step in range(1, chips):
        new_a = lax.ppermute(b, "tgt", a_pairs)
        if step < chips - 1:
            new_b = lax.ppermute(a, "tgt", b_pairs)
            b_side.append(new_b)
            b = new_b
        a = new_a
        a_side.append(new_a)
    parts = []
    for part in b_side[::-1] + [s_dense] + a_side:
        parts += [part, lax.ppermute(part, "tgt", cores)]
    return parts


def local(n_src, chips, tgt_weight, src_weight, coupling, block_tgt, block_src, block_cone, block_count, tgt_transfer):
    row, col = lax.axis_index("tgt"), lax.axis_index("src")
    t_clu, t_cones = tgt_weight.shape[0], tgt_weight.shape[1]
    s_clu, s_cones = src_weight.shape[0], src_weight.shape[1]
    t_dense, s_dense = prep(tgt_weight, src_weight)
    t_parts, relative = gather_row(t_dense, n_src)
    s_parts = gather_column(s_dense, chips)
    new_transfer = transfer(t_dense, tgt_transfer)

    tloc = jnp.clip(block_tgt - row * t_clu, 0, t_clu - 1)
    sloc = jnp.clip(block_src - col * s_clu, 0, s_clu - 1)
    owner = block_cone // t_cones
    part = (owner ^ col) if relative else owner
    tid = (part * t_clu + tloc) * t_cones + block_cone % t_cones
    owner = block_cone // s_cones
    z = row // 2
    ahead = (owner // 2 - z) * (1 - 2 * (z % 2))
    part = (ahead + chips - 2) * 2 + ((owner ^ row) & 1)
    sid = (part * s_clu + sloc) * s_cones + block_cone % s_cones
    new_coupling = main(coupling, tid, sid, block_count, t_parts, s_parts)
    return new_coupling, new_transfer


def solution(mesh):
    n_src, chips = mesh.shape["src"], mesh.shape["tgt"] // 2
    both = ("tgt", "src")
    return jax.shard_map(
        functools.partial(local, n_src, chips),
        mesh=mesh,
        in_specs=(
            P("tgt", "src", None),
            P("src", "tgt", None),
            P(both, None),
            P(both),
            P(both),
            P(both),
            P(both),
            P("tgt", "src", None),
        ),
        out_specs=(P(both, None), P("tgt", "src", None)),
        check_vma=False,
    )
```

```python
import functools

import jax
import jax.numpy as jnp
from jax import lax
from jax.experimental import pallas as pl
from jax.experimental.pallas import tpu as pltpu
from jax.sharding import PartitionSpec as P

W = 64
WW = 4096
CONES = 16
H = W // 2
LANES = 2 * W
CHUNKS = WW // LANES
PITCH = H + 1
GROUP = 16
f32, bf16 = jnp.float32, jnp.bfloat16
LATE_GROUP = 32
SMALL, LARGE = 12 * 2**20, 60 * 2**20


def swap_halves(x):
    return jnp.concatenate([x[:, W:], x[:, :W]], axis=1)


def low_lanes():
    return lax.broadcasted_iota(jnp.int32, (H, LANES), 1) < W


def left_product(t, c, low):
    lhs = jnp.concatenate([t[:, :W], t[:, W:]], axis=0)
    rhs = jnp.concatenate([c, swap_halves(c)], axis=0)
    y = jnp.dot(lhs, rhs, preferred_element_type=f32)
    return jnp.where(low, y[:H], y[H:])


def right_product(left, s, low):
    lhs = jnp.concatenate([left[:, :W], left[:, W:]], axis=0).astype(bf16)
    turned = swap_halves(s)
    rhs = jnp.concatenate([jnp.where(low, s, turned), jnp.where(low, turned, s)], axis=0)
    y = jnp.dot(lhs, rhs, preferred_element_type=f32)
    return jnp.where(low, y[:H], y[H:])


def rows_of(array):
    n, cones, _ = array.shape
    return array.reshape(n, cones, CHUNKS, LANES).transpose(0, 2, 1, 3).reshape(n, CHUNKS * cones, LANES)


def rows_back(rows, cones):
    n = rows.shape[0]
    return rows.reshape(n, CHUNKS, cones, LANES).transpose(0, 2, 1, 3).reshape(n, cones, WW)


def slot_rows(array):
    n = array.shape[0]
    return array.reshape(n // 8, 8, CHUNKS, LANES).transpose(0, 2, 1, 3).reshape(n * CHUNKS, LANES)


def slot_rows_back(rows):
    n = rows.shape[0] // CHUNKS
    return rows.reshape(n // 8, CHUNKS, 8, LANES).transpose(0, 2, 1, 3).reshape(n, WW)


def every(start, count, pitch):
    return pl.ds(start, count) if pitch == 1 else pl.ds(start, count, stride=pitch)


WHOLE = pl.BlockSpec(memory_space=pltpu.VMEM)
ANYWHERE = pl.BlockSpec(memory_space=pl.ANY)
IN_HBM = pl.BlockSpec(memory_space=pltpu.HBM)
SCALARS = pl.BlockSpec(memory_space=pltpu.SMEM)


def prep_src_kernel(cones, s_ref, s_out, scr):
    row = lax.broadcasted_iota(jnp.int32, (LANES, 4 * LANES), 0)
    lane = lax.broadcasted_iota(jnp.int32, (LANES, 4 * LANES), 1)
    same = (row // H) == (lane // LANES)
    even = jnp.where(same & (lane % W == 2 * (row % H)), 1.0, 0.0).astype(bf16)
    odd = jnp.where(same & (lane % W == 2 * (row % H) + 1), 1.0, 0.0).astype(bf16)
    low = low_lanes()
    rows = CHUNKS * cones
    clusters = 8 // cones

    def turn(i, carry):
        for u in range(clusters):
            scr[u * rows:(u + 1) * rows, :] = s_ref[i * clusters + u].astype(f32)
        blocks = [scr[every(u * rows + k, H, cones), :] for u in range(clusters) for k in range(cones)]
        for half in range(2):
            up = jnp.concatenate(blocks[4 * half:4 * half + 4], axis=0).T.astype(bf16)
            both = jnp.dot(up[:W], even, preferred_element_type=f32) + jnp.dot(
                up[W:], odd, preferred_element_type=f32
            )
            for m in range(4):
                d = both[:, m * LANES:(m + 1) * LANES]
                s_out[i * 8 + 4 * half + m] = jnp.where(low, d[:H], d[H:]).astype(bf16)
        return carry

    lax.fori_loop(0, s_out.shape[0] // 8, turn, 0, unroll=2)


def prep_src(src_weight):
    n, cones = src_weight.shape[0], src_weight.shape[1]
    return pl.pallas_call(
        functools.partial(prep_src_kernel, cones),
        in_specs=[WHOLE],
        out_specs=WHOLE,
        out_shape=jax.ShapeDtypeStruct((n * cones, H, LANES), bf16),
        scratch_shapes=[pltpu.VMEM((8 * H, LANES), f32)],
        compiler_params=pltpu.CompilerParams(vmem_limit_bytes=SMALL),
    )(rows_of(src_weight))


def prep_tgt_kernel(cones, t_ref, first_out, second_out, scr):
    row = lax.broadcasted_iota(jnp.int32, (LANES, LANES), 0)
    lane = lax.broadcasted_iota(jnp.int32, (LANES, LANES), 1)
    g, at = lane // W, lane % W
    odd_col = (at // H) ^ g
    order = jnp.where(row == g * W + 2 * (at % H) + odd_col, 1.0, 0.0).astype(bf16)
    rows = CHUNKS * cones
    half = t_ref.shape[0] // 2

    def sort(i, carry):
        for u, out in enumerate((first_out, second_out)):
            scr[u * rows:(u + 1) * rows, :] = jnp.dot(
                t_ref[u * half + i], order, preferred_element_type=f32
            )
            for k in range(cones):
                out[i * cones + k] = scr[every(u * rows + k, H, cones), :].astype(bf16)
        return carry

    lax.fori_loop(0, half, sort, 0, unroll=2)


def prep_tgt(tgt_weight):
    n, cones = tgt_weight.shape[0], tgt_weight.shape[1]
    half = jax.ShapeDtypeStruct((n * cones // 2, H, LANES), bf16)
    return pl.pallas_call(
        functools.partial(prep_tgt_kernel, cones),
        in_specs=[WHOLE],
        out_specs=[WHOLE, WHOLE],
        out_shape=[half, half],
        scratch_shapes=[pltpu.VMEM((2 * CHUNKS * cones, LANES), f32)],
        compiler_params=pltpu.CompilerParams(vmem_limit_bytes=SMALL),
    )(rows_of(tgt_weight))


def transfer_kernel(cones, late_from, t0_ref, t1_ref, x_ref, tid, live, o_ref, late, late_count, x_scr, o_scr):
    low = low_lanes()
    rows = CHUNKS * cones
    half = x_ref.shape[0] // 2

    def one(i, carry):
        for u, t_ref in enumerate((t0_ref, t1_ref)):
            at = u * half + i
            x_scr[u * rows:(u + 1) * rows, :] = x_ref[at].astype(f32)
            for k in range(cones):
                x = x_scr[every(u * rows + k, H, cones), :].astype(bf16)
                o_scr[every(u * rows + k, H, cones), :] = left_product(t_ref[i * cones + k], x, low)
            o_ref[at] = o_scr[u * rows:(u + 1) * rows, :].astype(bf16)
        return carry

    lax.fori_loop(0, half, one, 0, unroll=2)
    slots = tid.shape[0]

    def note(n, count):
        late[count] = n
        return count + jnp.where((tid[n] >= late_from) & (n < live[0]), 1, 0)

    count = lax.fori_loop(0, slots, note, 0, unroll=8)
    late_count[0] = count

    def pad(n, carry):
        late[count + n] = slots
        return carry

    lax.fori_loop(0, LATE_GROUP, pad, 0)


def transfer(halves, tgt_transfer, tid, live, late_from):
    cones = tgt_transfer.shape[1]
    rows = rows_of(tgt_transfer)
    slots = tid.shape[0]
    out, late, count = pl.pallas_call(
        functools.partial(transfer_kernel, cones, late_from),
        in_specs=[WHOLE, WHOLE, WHOLE, SCALARS, SCALARS],
        out_specs=[WHOLE, SCALARS, SCALARS],
        out_shape=[
            jax.ShapeDtypeStruct(rows.shape, bf16),
            jax.ShapeDtypeStruct((slots + LATE_GROUP,), jnp.int32),
            jax.ShapeDtypeStruct((1,), jnp.int32),
        ],
        scratch_shapes=[pltpu.VMEM((2 * CHUNKS * cones, LANES), f32)] * 2,
        compiler_params=pltpu.CompilerParams(vmem_limit_bytes=LARGE),
        cost_estimate=pl.CostEstimate(flops=2 * rows.size * W, bytes_accessed=12 * rows.size, transcendentals=0),
    )(*halves, rows, tid, live)
    return rows_back(out, cones), late, count


def load_table(parts, table, sem):
    copies, at = [], 0
    for part in parts:
        copies.append(pltpu.make_async_copy(part, table.at[pl.ds(at, part.shape[0])], sem.at[len(copies)]))
        at += part.shape[0]
    return copies


def for_each(count, act):
    def one(at, carry):
        act(at)
        return carry

    lax.fori_loop(0, count, one, 0)


def left_kernel(n_parts, block, late_from, tid, live, c_ref, *refs):
    parts = refs[:n_parts]
    o_ref, table, c_all, scr, sem, c_sem = refs[n_parts:]
    step_at, steps = pl.program_id(0), pl.num_programs(0)
    first = step_at * block
    low = low_lanes()
    rows = block * CHUNKS

    def block_copy(at):
        piece = pl.ds(pl.multiple_of(at * rows, rows), rows)
        return pltpu.make_async_copy(c_ref.at[piece], c_all.at[piece], c_sem.at[at])

    @pl.when(step_at == 0)
    def _():
        copies = load_table(parts, table, sem)
        for copy in copies:
            copy.start()
        for_each(steps, lambda at: block_copy(at).start())
        for copy in copies:
            copy.wait()

    block_copy(step_at).wait()

    def step(i, carry):
        i0 = pl.multiple_of(i * GROUP, GROUP)
        n0 = first + i0
        base = pl.multiple_of(n0 * CHUNKS, GROUP * CHUNKS)
        for u in range(GROUP // 8):
            for c in range(0, CHUNKS, 2):
                x = c_all[pl.ds(base + (u * CHUNKS + c) * 8, 16), :].astype(f32)
                scr[pl.ds(u * 8 * PITCH + c, 8, stride=PITCH), :] = x[:8]
                scr[pl.ds(u * 8 * PITCH + c + 1, 8, stride=PITCH), :] = x[8:]
        for n in range(GROUP):
            c = scr[n * PITCH:n * PITCH + H, :].astype(bf16)
            t = tid[n0 + n]
            product = left_product(table[jnp.minimum(t, late_from - 1)], c, low).astype(bf16)
            o_ref[i0 + n] = jnp.where(t < late_from, product, c)
        return carry

    @pl.when(first < live[0])
    def _():
        lax.fori_loop(0, block // GROUP, step, 0, unroll=8)


def left(coupling, tid, live, parts, late_from):
    slots = coupling.shape[0]
    block = 128
    entries = sum(p.shape[0] for p in parts)
    return pl.pallas_call(
        functools.partial(left_kernel, len(parts), block, late_from),
        grid_spec=pltpu.PrefetchScalarGridSpec(
            num_scalar_prefetch=2,
            grid=(slots // block,),
            in_specs=[IN_HBM] + [ANYWHERE] * len(parts),
            out_specs=pl.BlockSpec((block, H, LANES), lambda g, *_: (g, 0, 0)),
            scratch_shapes=[
                pltpu.VMEM((entries, H, LANES), bf16),
                pltpu.VMEM((slots * CHUNKS, LANES), bf16),
                pltpu.VMEM((GROUP * PITCH, LANES), f32),
                pltpu.SemaphoreType.DMA((len(parts),)),
                pltpu.SemaphoreType.DMA((slots // block,)),
            ],
        ),
        out_shape=jax.ShapeDtypeStruct((slots, H, LANES), bf16),
        compiler_params=pltpu.CompilerParams(vmem_limit_bytes=LARGE),
        cost_estimate=pl.CostEstimate(
            flops=8 * coupling.size * W, bytes_accessed=8 * coupling.size, transcendentals=0
        ),
    )(tid, live, slot_rows(coupling), *parts)


def right_kernel(
    n_late, n_parts, chips, block, late_from, tid, sid, live, late, late_count, chip, left_ref, *refs
):
    late_parts, parts = refs[:n_late], refs[n_late:n_late + n_parts]
    o_ref, left_all, late_table, table, out_all, scr = refs[n_late + n_parts:-4]
    sem, late_sem, l_sem, o_sem = refs[-4:]
    low = low_lanes()
    slots = tid.shape[0]
    rows = block * CHUNKS
    blocks = (live[0] + block - 1) // block

    def left_copy(at):
        piece = pl.ds(pl.multiple_of(at * block, block), block)
        return pltpu.make_async_copy(left_ref.at[piece], left_all.at[piece], l_sem.at[at])

    def out_copy(at):
        piece = pl.ds(pl.multiple_of(at * rows, rows), rows)
        return pltpu.make_async_copy(out_all.at[piece], o_ref.at[piece], o_sem.at[at])

    def here(at):
        far = at // 2 + 2 - chips
        there = jnp.where(chip[0] % 2 == 0, chip[0] + far, chip[0] - far)
        return (there >= 0) & (there < chips)

    last = load_table(late_parts, late_table, late_sem)
    columns = load_table(parts, table, sem)
    for copy in last:
        copy.start()
    for_each(blocks, lambda at: left_copy(at).start())
    for at, copy in enumerate(columns):
        pl.when(here(at))(copy.start)

    def clear(at):
        at = blocks + at
        out_all[pl.ds(pl.multiple_of(at * rows, rows), rows), :] = jnp.zeros((rows, LANES), bf16)
        out_copy(at).start()

    for_each(slots // block - blocks, clear)
    for copy in last:
        copy.wait()
    for_each(blocks, lambda at: left_copy(at).wait())

    if n_late:
        def fill(i):
            which = [late[i * LATE_GROUP + n] for n in range(LATE_GROUP)]
            held = [left_all[w] for w in which]
            done = []
            for w, c in zip(which, held):
                t = jnp.maximum(tid[jnp.minimum(w, slots - 1)] - late_from, 0)
                done.append(left_product(late_table[t], c, low).astype(bf16))
            for w, product in zip(which, done):
                left_all[w] = product

        for_each((late_count[0] + LATE_GROUP - 1) // LATE_GROUP, fill)
    for at, copy in enumerate(columns):
        pl.when(here(at))(copy.wait)

    def step(i, carry):
        n0 = pl.multiple_of(i * GROUP, GROUP)
        for n in range(GROUP):
            scr[n * PITCH:n * PITCH + H, :] = right_product(left_all[n0 + n], table[sid[n0 + n]], low)
        keep = lax.broadcasted_iota(jnp.int32, (8, LANES), 0) + n0
        base = pl.multiple_of(n0 * CHUNKS, GROUP * CHUNKS)
        for u in range(GROUP // 8):
            mask = keep + u * 8 < live[0]
            for c in range(0, CHUNKS, 2):
                pair = [
                    jnp.where(mask, scr[pl.ds(u * 8 * PITCH + c + e, 8, stride=PITCH), :], 0.0)
                    for e in range(2)
                ]
                out_all[pl.ds(base + (u * CHUNKS + c) * 8, 16), :] = jnp.concatenate(pair, axis=0).astype(bf16)
        return carry

    per = block // GROUP

    def work(at):
        lax.fori_loop(0, per, lambda i, carry: step(at * per + i, carry), 0, unroll=8)
        out_copy(at).start()

    for_each(blocks, work)
    for_each(slots // block, lambda at: out_copy(at).wait())


def right(left_all, tid, sid, live, late, late_count, chip, late_parts, parts, late_from, chips):
    slots = left_all.shape[0]
    block = 128 if slots % 128 == 0 else GROUP
    n_late, entries = sum(p.shape[0] for p in late_parts), sum(p.shape[0] for p in parts)
    rows = pl.pallas_call(
        functools.partial(right_kernel, len(late_parts), len(parts), chips, block, late_from),
        in_specs=[SCALARS] * 6 + [ANYWHERE] * (1 + len(late_parts) + len(parts)),
        out_specs=ANYWHERE,
        scratch_shapes=[
            pltpu.VMEM((slots + 1, H, LANES), bf16),
            pltpu.VMEM((max(n_late, 8), H, LANES), bf16),
            pltpu.VMEM((entries, H, LANES), bf16),
            pltpu.VMEM((slots * CHUNKS, LANES), bf16),
            pltpu.VMEM((GROUP * PITCH, LANES), f32),
            pltpu.SemaphoreType.DMA((len(parts),)),
            pltpu.SemaphoreType.DMA((max(len(late_parts), 1),)),
            pltpu.SemaphoreType.DMA((slots // block,)),
            pltpu.SemaphoreType.DMA((slots // block,)),
        ],
        out_shape=jax.ShapeDtypeStruct((slots * CHUNKS, LANES), bf16),
        compiler_params=pltpu.CompilerParams(vmem_limit_bytes=LARGE),
    )(tid, sid, live, late, late_count, chip, left_all, *late_parts, *parts)
    return slot_rows_back(rows)


def along_x(part):
    return lax.ppermute(part, "src", [(i, i ^ 1) for i in range(4)])


def along_y(part):
    return lax.ppermute(part, "src", [(i, i ^ 2) for i in range(4)])


def column_pairs(chips):
    def far(z):
        return z if z in (0, chips - 1) else ((z - 1) ^ 1) + 1

    near_pairs = [(2 * z + c, 2 * (z ^ 1) + c) for z in range(chips) for c in range(2)]
    far_pairs = [(2 * z + c, 2 * far(z) + c) for z in range(chips) for c in range(2)]
    return near_pairs, far_pairs, [(i, i ^ 1) for i in range(2 * chips)]


def send(part, pairs):
    return lax.ppermute(part, "tgt", pairs)


def slot_tables(n_src, chips, row, col, t_shape, s_shape, block_tgt, block_src, block_cone):
    t_clu, t_cones = t_shape
    s_clu, s_cones = s_shape
    tloc = jnp.clip(block_tgt - row * t_clu, 0, t_clu - 1)
    sloc = jnp.clip(block_src - col * s_clu, 0, s_clu - 1)
    owner = block_cone // t_cones
    if n_src == 4:
        tid = ((owner ^ col) * t_clu + tloc) * t_cones + block_cone % t_cones
        late_from = 3 * t_clu * t_cones
    else:
        half = t_clu // 2
        tid = ((tloc // half * n_src + owner) * half + tloc % half) * t_cones + block_cone % t_cones
        late_from = n_src * t_clu * t_cones
    owner = block_cone // s_cones
    z = row // 2
    ahead = (owner // 2 - z) * (1 - 2 * (z % 2))
    part = (ahead + chips - 2) * 2 + ((owner ^ row) & 1)
    return tid, late_from, (part * s_clu + sloc) * s_cones + block_cone % s_cones


def local(n_src, chips, tgt_weight, src_weight, coupling, block_tgt, block_src, block_cone, block_count, tgt_transfer):
    row, col = lax.axis_index("tgt"), lax.axis_index("src")
    near, far, cores = column_pairs(chips)
    fence = lax.optimization_barrier
    square = n_src == 4
    t_shape, s_shape = tgt_weight.shape[:2], src_weight.shape[:2]

    s_dense = prep_src(src_weight)
    a, b = send(s_dense, near), send(s_dense, far)
    own = [s_dense, send(s_dense, cores)]
    halves = prep_tgt(tgt_weight)
    slots = (block_tgt, block_src, block_cone)
    a, b, own, tgt_transfer, slots = fence((a, b, own, tgt_transfer, slots))
    if square:
        x0, y1 = along_x(halves[0]), along_y(halves[1])
        x0, y1, halves = fence((x0, y1, halves))
        x1, y0 = along_x(halves[1]), along_y(halves[0])
    else:
        gathered = [lax.all_gather(h, "src", axis=0).reshape(-1, H, LANES) for h in halves]

    tid, late_from, sid = slot_tables(n_src, chips, row, col, t_shape, s_shape, *slots)
    new_transfer, late, late_count = transfer(halves, tgt_transfer, tid, block_count, late_from)
    ahead_parts, behind_parts = [], []
    for step in range(2, chips):
        kept_a, kept_b, late = fence((a, b, late)) if step == 2 else (a, b, late)
        ahead_parts.append([kept_a, send(kept_a, cores)])
        behind_parts.append([kept_b, send(kept_b, cores)])
        a, b = send(b, near), send(a, far) if step < chips - 1 else None
        if step == 2 and square:
            x0, y1, x1, y0, a, b, ahead_parts, behind_parts, coupling, late, sid = fence(
                (x0, y1, x1, y0, a, b, ahead_parts, behind_parts, coupling, late, sid)
            )
            d0, d1 = along_y(x0), along_x(y1)

    t_parts, late_parts = ([*halves, x0, x1, y0, y1], [d0, d1]) if square else (gathered, [])
    left_all = left(coupling, tid, block_count, t_parts, late_from)
    a, late_parts, left_all, ahead_parts, behind_parts = fence((a, late_parts, left_all, ahead_parts, behind_parts))
    ahead_parts.append([a, send(a, cores)])
    s_parts = sum(behind_parts[::-1] + [own] + ahead_parts, [])
    chip = (row // 2).reshape(1)
    new_coupling = right(
        left_all, tid, sid, block_count, late, late_count, chip, late_parts, s_parts, late_from, chips
    )
    return new_coupling, new_transfer


def solution(mesh):
    n_src, chips = mesh.shape["src"], mesh.shape["tgt"] // 2
    both = ("tgt", "src")
    return jax.shard_map(
        functools.partial(local, n_src, chips),
        mesh=mesh,
        in_specs=(
            P("tgt", "src", None),
            P("src", "tgt", None),
            P(both, None),
            P(both),
            P(both),
            P(both),
            P(both),
            P("tgt", "src", None),
        ),
        out_specs=(P(both, None), P("tgt", "src", None)),
        check_vma=False,
    )
```

```python
import functools

import jax
import jax.numpy as jnp
from jax import lax
from jax.experimental import pallas as pl
from jax.experimental.pallas import tpu as pltpu
from jax.sharding import PartitionSpec as P

W = 64
WW = 4096
CONES = 16
H = W // 2
LANES = 2 * W
CHUNKS = WW // LANES
PITCH = H + 1
GROUP = 16
f32, bf16 = jnp.float32, jnp.bfloat16
LATE_GROUP = 32
SMALL, LARGE = 12 * 2**20, 60 * 2**20


def swap_halves(x):
    return jnp.concatenate([x[:, W:], x[:, :W]], axis=1)


def low_lanes():
    return lax.broadcasted_iota(jnp.int32, (H, LANES), 1) < W


def left_product(t, c, low):
    lhs = jnp.concatenate([t[:, :W], t[:, W:]], axis=0)
    rhs = jnp.concatenate([c, swap_halves(c)], axis=0)
    y = jnp.dot(lhs, rhs, preferred_element_type=f32)
    return jnp.where(low, y[:H], y[H:])


def right_product(left, s, low):
    lhs = jnp.concatenate([left[:, :W], left[:, W:]], axis=0).astype(bf16)
    turned = swap_halves(s)
    rhs = jnp.concatenate([jnp.where(low, s, turned), jnp.where(low, turned, s)], axis=0)
    y = jnp.dot(lhs, rhs, preferred_element_type=f32)
    return jnp.where(low, y[:H], y[H:])


def rows_of(array):
    n, cones, _ = array.shape
    return array.reshape(n, cones, CHUNKS, LANES).transpose(0, 2, 1, 3).reshape(n, CHUNKS * cones, LANES)


def rows_back(rows, cones):
    n = rows.shape[0]
    return rows.reshape(n, CHUNKS, cones, LANES).transpose(0, 2, 1, 3).reshape(n, cones, WW)


def slot_rows(array):
    n = array.shape[0]
    return array.reshape(n // 8, 8, CHUNKS, LANES).transpose(0, 2, 1, 3).reshape(n * CHUNKS, LANES)


def slot_rows_back(rows):
    n = rows.shape[0] // CHUNKS
    return rows.reshape(n // 8, CHUNKS, 8, LANES).transpose(0, 2, 1, 3).reshape(n, WW)


def every(start, count, pitch):
    return pl.ds(start, count) if pitch == 1 else pl.ds(start, count, stride=pitch)


WHOLE = pl.BlockSpec(memory_space=pltpu.VMEM)
ANYWHERE = pl.BlockSpec(memory_space=pl.ANY)
IN_HBM = pl.BlockSpec(memory_space=pltpu.HBM)
SCALARS = pl.BlockSpec(memory_space=pltpu.SMEM)


def prep_src_kernel(cones, s_ref, s_out, scr):
    row = lax.broadcasted_iota(jnp.int32, (LANES, 4 * LANES), 0)
    lane = lax.broadcasted_iota(jnp.int32, (LANES, 4 * LANES), 1)
    same = (row // H) == (lane // LANES)
    even = jnp.where(same & (lane % W == 2 * (row % H)), 1.0, 0.0).astype(bf16)
    odd = jnp.where(same & (lane % W == 2 * (row % H) + 1), 1.0, 0.0).astype(bf16)
    low = low_lanes()
    rows = CHUNKS * cones
    clusters = 8 // cones

    def turn(i, carry):
        for u in range(clusters):
            scr[u * rows:(u + 1) * rows, :] = s_ref[i * clusters + u].astype(f32)
        blocks = [scr[every(u * rows + k, H, cones), :] for u in range(clusters) for k in range(cones)]
        for half in range(2):
            up = jnp.concatenate(blocks[4 * half:4 * half + 4], axis=0).T.astype(bf16)
            both = jnp.dot(up[:W], even, preferred_element_type=f32) + jnp.dot(
                up[W:], odd, preferred_element_type=f32
            )
            for m in range(4):
                d = both[:, m * LANES:(m + 1) * LANES]
                s_out[i * 8 + 4 * half + m] = jnp.where(low, d[:H], d[H:]).astype(bf16)
        return carry

    lax.fori_loop(0, s_out.shape[0] // 8, turn, 0, unroll=2)


def prep_src(src_weight):
    n, cones = src_weight.shape[0], src_weight.shape[1]
    return pl.pallas_call(
        functools.partial(prep_src_kernel, cones),
        in_specs=[WHOLE],
        out_specs=WHOLE,
        out_shape=jax.ShapeDtypeStruct((n * cones, H, LANES), bf16),
        scratch_shapes=[pltpu.VMEM((8 * H, LANES), f32)],
        compiler_params=pltpu.CompilerParams(vmem_limit_bytes=SMALL),
    )(rows_of(src_weight))


def prep_tgt_kernel(cones, t_ref, first_out, second_out, scr):
    row = lax.broadcasted_iota(jnp.int32, (LANES, LANES), 0)
    lane = lax.broadcasted_iota(jnp.int32, (LANES, LANES), 1)
    g, at = lane // W, lane % W
    odd_col = (at // H) ^ g
    order = jnp.where(row == g * W + 2 * (at % H) + odd_col, 1.0, 0.0).astype(bf16)
    rows = CHUNKS * cones
    half = t_ref.shape[0] // 2

    def sort(i, carry):
        for u, out in enumerate((first_out, second_out)):
            scr[u * rows:(u + 1) * rows, :] = jnp.dot(
                t_ref[u * half + i], order, preferred_element_type=f32
            )
            for k in range(cones):
                out[i * cones + k] = scr[every(u * rows + k, H, cones), :].astype(bf16)
        return carry

    lax.fori_loop(0, half, sort, 0, unroll=2)


def prep_tgt(tgt_weight):
    n, cones = tgt_weight.shape[0], tgt_weight.shape[1]
    half = jax.ShapeDtypeStruct((n * cones // 2, H, LANES), bf16)
    return pl.pallas_call(
        functools.partial(prep_tgt_kernel, cones),
        in_specs=[WHOLE],
        out_specs=[WHOLE, WHOLE],
        out_shape=[half, half],
        scratch_shapes=[pltpu.VMEM((2 * CHUNKS * cones, LANES), f32)],
        compiler_params=pltpu.CompilerParams(vmem_limit_bytes=SMALL),
    )(rows_of(tgt_weight))


def transfer_kernel(cones, late_from, t0_ref, t1_ref, x_ref, tid, live, o_ref, late, late_count, x_scr, o_scr):
    low = low_lanes()
    rows = CHUNKS * cones
    half = x_ref.shape[0] // 2

    def one(i, carry):
        for u, t_ref in enumerate((t0_ref, t1_ref)):
            at = u * half + i
            x_scr[u * rows:(u + 1) * rows, :] = x_ref[at].astype(f32)
            for k in range(cones):
                x = x_scr[every(u * rows + k, H, cones), :].astype(bf16)
                o_scr[every(u * rows + k, H, cones), :] = left_product(t_ref[i * cones + k], x, low)
            o_ref[at] = o_scr[u * rows:(u + 1) * rows, :].astype(bf16)
        return carry

    lax.fori_loop(0, half, one, 0, unroll=2)
    slots = tid.shape[0]

    def note(n, count):
        late[count] = n
        return count + jnp.where((tid[n] >= late_from) & (n < live[0]), 1, 0)

    count = lax.fori_loop(0, slots, note, 0, unroll=8)
    late_count[0] = count

    def pad(n, carry):
        late[count + n] = slots
        return carry

    lax.fori_loop(0, LATE_GROUP, pad, 0)


def transfer(halves, tgt_transfer, tid, live, late_from):
    cones = tgt_transfer.shape[1]
    rows = rows_of(tgt_transfer)
    slots = tid.shape[0]
    out, late, count = pl.pallas_call(
        functools.partial(transfer_kernel, cones, late_from),
        in_specs=[WHOLE, WHOLE, WHOLE, SCALARS, SCALARS],
        out_specs=[WHOLE, SCALARS, SCALARS],
        out_shape=[
            jax.ShapeDtypeStruct(rows.shape, bf16),
            jax.ShapeDtypeStruct((slots + LATE_GROUP,), jnp.int32),
            jax.ShapeDtypeStruct((1,), jnp.int32),
        ],
        scratch_shapes=[pltpu.VMEM((2 * CHUNKS * cones, LANES), f32)] * 2,
        compiler_params=pltpu.CompilerParams(vmem_limit_bytes=24 * 2**20),
        cost_estimate=pl.CostEstimate(flops=2 * rows.size * W, bytes_accessed=12 * rows.size, transcendentals=0),
    )(*halves, rows, tid, live)
    return rows_back(out, cones), late, count


def load_table(parts, table, sem):
    copies, at = [], 0
    for part in parts:
        copies.append(pltpu.make_async_copy(part, table.at[pl.ds(at, part.shape[0])], sem.at[len(copies)]))
        at += part.shape[0]
    return copies


def for_each(count, act):
    def one(at, carry):
        act(at)
        return carry

    lax.fori_loop(0, count, one, 0)


def left_kernel(n_parts, block, late_from, tid, live, c_ref, *refs):
    parts = refs[:n_parts]
    o_ref, table, c_all, scr, sem, c_sem = refs[n_parts:]
    step_at, steps = pl.program_id(0), pl.num_programs(0)
    first = step_at * block
    low = low_lanes()
    rows = block * CHUNKS

    def block_copy(at):
        piece = pl.ds(pl.multiple_of(at * rows, rows), rows)
        return pltpu.make_async_copy(c_ref.at[piece], c_all.at[piece], c_sem.at[at])

    @pl.when(step_at == 0)
    def _():
        copies = load_table(parts, table, sem)
        for copy in copies:
            copy.start()
        for_each(steps, lambda at: block_copy(at).start())
        for copy in copies:
            copy.wait()

    block_copy(step_at).wait()

    def step(i, carry):
        i0 = pl.multiple_of(i * GROUP, GROUP)
        n0 = first + i0
        base = pl.multiple_of(n0 * CHUNKS, GROUP * CHUNKS)
        for u in range(GROUP // 8):
            for c in range(0, CHUNKS, 2):
                x = c_all[pl.ds(base + (u * CHUNKS + c) * 8, 16), :].astype(f32)
                scr[pl.ds(u * 8 * PITCH + c, 8, stride=PITCH), :] = x[:8]
                scr[pl.ds(u * 8 * PITCH + c + 1, 8, stride=PITCH), :] = x[8:]
        for n in range(GROUP):
            c = scr[n * PITCH:n * PITCH + H, :].astype(bf16)
            t = tid[n0 + n]
            product = left_product(table[jnp.minimum(t, late_from - 1)], c, low).astype(bf16)
            o_ref[i0 + n] = jnp.where(t < late_from, product, c)
        return carry

    @pl.when(first < live[0])
    def _():
        lax.fori_loop(0, block // GROUP, step, 0, unroll=8)


def left(coupling, tid, live, parts, late_from):
    slots = coupling.shape[0]
    block = 128
    entries = sum(p.shape[0] for p in parts)
    return pl.pallas_call(
        functools.partial(left_kernel, len(parts), block, late_from),
        grid_spec=pltpu.PrefetchScalarGridSpec(
            num_scalar_prefetch=2,
            grid=(slots // block,),
            in_specs=[IN_HBM] + [ANYWHERE] * len(parts),
            out_specs=pl.BlockSpec((block, H, LANES), lambda g, *_: (g, 0, 0)),
            scratch_shapes=[
                pltpu.VMEM((entries, H, LANES), bf16),
                pltpu.VMEM((slots * CHUNKS, LANES), bf16),
                pltpu.VMEM((GROUP * PITCH, LANES), f32),
                pltpu.SemaphoreType.DMA((len(parts),)),
                pltpu.SemaphoreType.DMA((slots // block,)),
            ],
        ),
        out_shape=jax.ShapeDtypeStruct((slots, H, LANES), bf16),
        compiler_params=pltpu.CompilerParams(vmem_limit_bytes=44 * 2**20),
        cost_estimate=pl.CostEstimate(
            flops=8 * coupling.size * W, bytes_accessed=8 * coupling.size, transcendentals=0
        ),
    )(tid, live, slot_rows(coupling), *parts)


def right_kernel(
    n_late, n_parts, chips, block, late_from, tid, sid, live, late, late_count, chip, left_ref, *refs
):
    late_parts, parts = refs[:n_late], refs[n_late:n_late + n_parts]
    o_ref, left_all, late_table, table, out_all, scr = refs[n_late + n_parts:-4]
    sem, late_sem, l_sem, o_sem = refs[-4:]
    low = low_lanes()
    slots = tid.shape[0]
    rows = block * CHUNKS
    blocks = (live[0] + block - 1) // block

    def left_copy(at):
        piece = pl.ds(pl.multiple_of(at * block, block), block)
        return pltpu.make_async_copy(left_ref.at[piece], left_all.at[piece], l_sem.at[at])

    def out_copy(at):
        piece = pl.ds(pl.multiple_of(at * rows, rows), rows)
        return pltpu.make_async_copy(out_all.at[piece], o_ref.at[piece], o_sem.at[at])

    def here(at):
        far = at // 2 + 2 - chips
        there = jnp.where(chip[0] % 2 == 0, chip[0] + far, chip[0] - far)
        return (there >= 0) & (there < chips)

    last = load_table(late_parts, late_table, late_sem)
    columns = load_table(parts, table, sem)
    for copy in last:
        copy.start()
    for_each(blocks, lambda at: left_copy(at).start())
    for at, copy in enumerate(columns):
        pl.when(here(at))(copy.start)

    def clear(at):
        at = blocks + at
        out_all[pl.ds(pl.multiple_of(at * rows, rows), rows), :] = jnp.zeros((rows, LANES), bf16)
        out_copy(at).start()

    for_each(slots // block - blocks, clear)
    for copy in last:
        copy.wait()
    for_each(blocks, lambda at: left_copy(at).wait())

    if n_late:
        def fill(i):
            which = [late[i * LATE_GROUP + n] for n in range(LATE_GROUP)]
            held = [left_all[w] for w in which]
            done = []
            for w, c in zip(which, held):
                t = jnp.maximum(tid[jnp.minimum(w, slots - 1)] - late_from, 0)
                done.append(left_product(late_table[t], c, low).astype(bf16))
            for w, product in zip(which, done):
                left_all[w] = product

        for_each((late_count[0] + LATE_GROUP - 1) // LATE_GROUP, fill)
    for at, copy in enumerate(columns):
        pl.when(here(at))(copy.wait)

    def step(i, carry):
        n0 = pl.multiple_of(i * GROUP, GROUP)
        for n in range(GROUP):
            scr[n * PITCH:n * PITCH + H, :] = right_product(left_all[n0 + n], table[sid[n0 + n]], low)
        keep = lax.broadcasted_iota(jnp.int32, (8, LANES), 0) + n0
        base = pl.multiple_of(n0 * CHUNKS, GROUP * CHUNKS)
        for u in range(GROUP // 8):
            mask = keep + u * 8 < live[0]
            for c in range(0, CHUNKS, 2):
                pair = [
                    jnp.where(mask, scr[pl.ds(u * 8 * PITCH + c + e, 8, stride=PITCH), :], 0.0)
                    for e in range(2)
                ]
                out_all[pl.ds(base + (u * CHUNKS + c) * 8, 16), :] = jnp.concatenate(pair, axis=0).astype(bf16)
        return carry

    per = block // GROUP

    def work(at):
        lax.fori_loop(0, per, lambda i, carry: step(at * per + i, carry), 0, unroll=8)
        out_copy(at).start()

    for_each(blocks, work)
    for_each(slots // block, lambda at: out_copy(at).wait())


def right(left_all, tid, sid, live, late, late_count, chip, late_parts, parts, late_from, chips):
    slots = left_all.shape[0]
    block = 128 if slots % 128 == 0 else GROUP
    n_late, entries = sum(p.shape[0] for p in late_parts), sum(p.shape[0] for p in parts)
    rows = pl.pallas_call(
        functools.partial(right_kernel, len(late_parts), len(parts), chips, block, late_from),
        in_specs=[SCALARS] * 6 + [ANYWHERE] * (1 + len(late_parts) + len(parts)),
        out_specs=ANYWHERE,
        scratch_shapes=[
            pltpu.VMEM((slots + 1, H, LANES), bf16),
            pltpu.VMEM((max(n_late, 8), H, LANES), bf16),
            pltpu.VMEM((entries, H, LANES), bf16),
            pltpu.VMEM((slots * CHUNKS, LANES), bf16),
            pltpu.VMEM((GROUP * PITCH, LANES), f32),
            pltpu.SemaphoreType.DMA((len(parts),)),
            pltpu.SemaphoreType.DMA((max(len(late_parts), 1),)),
            pltpu.SemaphoreType.DMA((slots // block,)),
            pltpu.SemaphoreType.DMA((slots // block,)),
        ],
        out_shape=jax.ShapeDtypeStruct((slots * CHUNKS, LANES), bf16),
        compiler_params=pltpu.CompilerParams(vmem_limit_bytes=30 * 2**20),
    )(tid, sid, live, late, late_count, chip, left_all, *late_parts, *parts)
    return slot_rows_back(rows)


def along_x(part):
    return lax.ppermute(part, "src", [(i, i ^ 1) for i in range(4)])


def along_y(part):
    return lax.ppermute(part, "src", [(i, i ^ 2) for i in range(4)])


def column_pairs(chips):
    def far(z):
        return z if z in (0, chips - 1) else ((z - 1) ^ 1) + 1

    near_pairs = [(2 * z + c, 2 * (z ^ 1) + c) for z in range(chips) for c in range(2)]
    far_pairs = [(2 * z + c, 2 * far(z) + c) for z in range(chips) for c in range(2)]
    return near_pairs, far_pairs, [(i, i ^ 1) for i in range(2 * chips)]


def send(part, pairs):
    return lax.ppermute(part, "tgt", pairs)


def slot_tables(n_src, chips, row, col, t_shape, s_shape, block_tgt, block_src, block_cone):
    t_clu, t_cones = t_shape
    s_clu, s_cones = s_shape
    tloc = jnp.clip(block_tgt - row * t_clu, 0, t_clu - 1)
    sloc = jnp.clip(block_src - col * s_clu, 0, s_clu - 1)
    owner = block_cone // t_cones
    if n_src == 4:
        tid = ((owner ^ col) * t_clu + tloc) * t_cones + block_cone % t_cones
        late_from = 3 * t_clu * t_cones
    else:
        half = t_clu // 2
        tid = ((tloc // half * n_src + owner) * half + tloc % half) * t_cones + block_cone % t_cones
        late_from = n_src * t_clu * t_cones
    owner = block_cone // s_cones
    z = row // 2
    ahead = (owner // 2 - z) * (1 - 2 * (z % 2))
    part = (ahead + chips - 2) * 2 + ((owner ^ row) & 1)
    return tid, late_from, (part * s_clu + sloc) * s_cones + block_cone % s_cones


def local(n_src, chips, tgt_weight, src_weight, coupling, block_tgt, block_src, block_cone, block_count, tgt_transfer):
    row, col = lax.axis_index("tgt"), lax.axis_index("src")
    near, far, cores = column_pairs(chips)
    fence = lax.optimization_barrier
    square = n_src == 4
    t_shape, s_shape = tgt_weight.shape[:2], src_weight.shape[:2]

    s_dense = prep_src(src_weight)
    a, b = send(s_dense, near), send(s_dense, far)
    own = [s_dense, send(s_dense, cores)]
    halves = prep_tgt(tgt_weight)
    slots = (block_tgt, block_src, block_cone)
    a, b, own, tgt_transfer, slots = fence((a, b, own, tgt_transfer, slots))
    if square:
        x0, y1 = along_x(halves[0]), along_y(halves[1])
        x0, y1, halves = fence((x0, y1, halves))
        x1, y0 = along_x(halves[1]), along_y(halves[0])
    else:
        gathered = [lax.all_gather(h, "src", axis=0).reshape(-1, H, LANES) for h in halves]

    tid, late_from, sid = slot_tables(n_src, chips, row, col, t_shape, s_shape, *slots)
    new_transfer, late, late_count = transfer(halves, tgt_transfer, tid, block_count, late_from)
    ahead_parts, behind_parts = [], []
    for step in range(2, chips):
        kept_a, kept_b, late = fence((a, b, late)) if step == 2 else (a, b, late)
        a, b = send(b, near), send(a, far) if step < chips - 1 else None
        if step == 3 and square:
            kept_a, kept_b = kept_x, kept_y
        ahead_parts.append([kept_a, send(kept_a, cores)])
        behind_parts.append([kept_b, send(kept_b, cores)])
        if step == 2 and square:
            a, b, late = fence((a, b, late))
            x0, y1, x1, y0, late, sid, kept_x, kept_y = fence((x0, y1, x1, y0, late, sid, a, b))
            d0, d1 = along_y(x0), along_x(y1)

    t_parts, late_parts = ([*halves, x0, x1, y0, y1], [d0, d1]) if square else (gathered, [])
    left_all = left(coupling, tid, block_count, t_parts, late_from)
    a, left_all = fence((a, left_all))
    ahead_parts.append([a, send(a, cores)])
    s_parts = sum(behind_parts[::-1] + [own] + ahead_parts, [])
    chip = (row // 2).reshape(1)
    new_coupling = right(
        left_all, tid, sid, block_count, late, late_count, chip, late_parts, s_parts, late_from, chips
    )
    return new_coupling, new_transfer


def solution(mesh):
    n_src, chips = mesh.shape["src"], mesh.shape["tgt"] // 2
    both = ("tgt", "src")
    return jax.shard_map(
        functools.partial(local, n_src, chips),
        mesh=mesh,
        in_specs=(
            P("tgt", "src", None),
            P("src", "tgt", None),
            P(both, None),
            P(both),
            P(both),
            P(both),
            P(both),
            P("tgt", "src", None),
        ),
        out_specs=(P(both, None), P("tgt", "src", None)),
        check_vma=False,
    )
```

```python
import functools

import jax
import jax.numpy as jnp
from jax import lax
from jax.experimental import pallas as pl
from jax.experimental.pallas import tpu as pltpu
from jax.sharding import PartitionSpec as P

W = 64
WW = 4096
CONES = 16
H = W // 2
LANES = 2 * W
CHUNKS = WW // LANES
PITCH = H + 1
GROUP = 16
f32, bf16 = jnp.float32, jnp.bfloat16
LATE_GROUP = 64
SMALL, LARGE = 12 * 2**20, 60 * 2**20


def swap_halves(x):
    return jnp.concatenate([x[:, W:], x[:, :W]], axis=1)


def low_lanes():
    return lax.broadcasted_iota(jnp.int32, (H, LANES), 1) < W


def left_product(t, c, low):
    lhs = jnp.concatenate([t[:, :W], t[:, W:]], axis=0)
    rhs = jnp.concatenate([c, swap_halves(c)], axis=0)
    y = jnp.dot(lhs, rhs, preferred_element_type=f32)
    return jnp.where(low, y[:H], y[H:])


def right_product(left, s, low):
    lhs = jnp.concatenate([left[:, :W], left[:, W:]], axis=0).astype(bf16)
    turned = swap_halves(s)
    rhs = jnp.concatenate([jnp.where(low, s, turned), jnp.where(low, turned, s)], axis=0)
    y = jnp.dot(lhs, rhs, preferred_element_type=f32)
    return jnp.where(low, y[:H], y[H:])


def rows_of(array):
    n, cones, _ = array.shape
    return array.reshape(n, cones, CHUNKS, LANES).transpose(0, 2, 1, 3).reshape(n, CHUNKS * cones, LANES)


def rows_back(rows, cones):
    n = rows.shape[0]
    return rows.reshape(n, CHUNKS, cones, LANES).transpose(0, 2, 1, 3).reshape(n, cones, WW)


def slot_rows(array):
    n = array.shape[0]
    return array.reshape(n // 8, 8, CHUNKS, LANES).transpose(0, 2, 1, 3).reshape(n * CHUNKS, LANES)


def slot_rows_back(rows):
    n = rows.shape[0] // CHUNKS
    return rows.reshape(n // 8, CHUNKS, 8, LANES).transpose(0, 2, 1, 3).reshape(n, WW)


def every(start, count, pitch):
    return pl.ds(start, count) if pitch == 1 else pl.ds(start, count, stride=pitch)


WHOLE = pl.BlockSpec(memory_space=pltpu.VMEM)
ANYWHERE = pl.BlockSpec(memory_space=pl.ANY)
IN_HBM = pl.BlockSpec(memory_space=pltpu.HBM)
SCALARS = pl.BlockSpec(memory_space=pltpu.SMEM)


def prep_src_kernel(cones, s_ref, s_out, scr):
    row = lax.broadcasted_iota(jnp.int32, (LANES, 4 * LANES), 0)
    lane = lax.broadcasted_iota(jnp.int32, (LANES, 4 * LANES), 1)
    same = (row // H) == (lane // LANES)
    even = jnp.where(same & (lane % W == 2 * (row % H)), 1.0, 0.0).astype(bf16)
    odd = jnp.where(same & (lane % W == 2 * (row % H) + 1), 1.0, 0.0).astype(bf16)
    low = low_lanes()
    rows = CHUNKS * cones
    clusters = 8 // cones

    def turn(i, carry):
        for u in range(clusters):
            scr[u * rows:(u + 1) * rows, :] = s_ref[i * clusters + u].astype(f32)
        blocks = [scr[every(u * rows + k, H, cones), :] for u in range(clusters) for k in range(cones)]
        for half in range(2):
            up = jnp.concatenate(blocks[4 * half:4 * half + 4], axis=0).T.astype(bf16)
            both = jnp.dot(up[:W], even, preferred_element_type=f32) + jnp.dot(
                up[W:], odd, preferred_element_type=f32
            )
            for m in range(4):
                d = both[:, m * LANES:(m + 1) * LANES]
                s_out[i * 8 + 4 * half + m] = jnp.where(low, d[:H], d[H:]).astype(bf16)
        return carry

    lax.fori_loop(0, s_out.shape[0] // 8, turn, 0, unroll=2)


def prep_src(src_weight):
    n, cones = src_weight.shape[0], src_weight.shape[1]
    return pl.pallas_call(
        functools.partial(prep_src_kernel, cones),
        in_specs=[WHOLE],
        out_specs=WHOLE,
        out_shape=jax.ShapeDtypeStruct((n * cones, H, LANES), bf16),
        scratch_shapes=[pltpu.VMEM((8 * H, LANES), f32)],
        compiler_params=pltpu.CompilerParams(vmem_limit_bytes=SMALL),
    )(rows_of(src_weight))


def prep_tgt_kernel(cones, t_ref, out, scr):
    row = lax.broadcasted_iota(jnp.int32, (LANES, LANES), 0)
    lane = lax.broadcasted_iota(jnp.int32, (LANES, LANES), 1)
    g, at = lane // W, lane % W
    odd_col = (at // H) ^ g
    order = jnp.where(row == g * W + 2 * (at % H) + odd_col, 1.0, 0.0).astype(bf16)
    rows = CHUNKS * cones

    def sort(i, carry):
        for u in range(2):
            at = 2 * i + u
            scr[u * rows:(u + 1) * rows, :] = jnp.dot(t_ref[at], order, preferred_element_type=f32)
            for k in range(cones):
                out[at * cones + k] = scr[every(u * rows + k, H, cones), :].astype(bf16)
        return carry

    lax.fori_loop(0, t_ref.shape[0] // 2, sort, 0, unroll=2)


def prep_tgt(tgt_weight):
    n, cones = tgt_weight.shape[0], tgt_weight.shape[1]
    return pl.pallas_call(
        functools.partial(prep_tgt_kernel, cones),
        in_specs=[WHOLE],
        out_specs=WHOLE,
        out_shape=jax.ShapeDtypeStruct((n * cones, H, LANES), bf16),
        scratch_shapes=[pltpu.VMEM((2 * CHUNKS * cones, LANES), f32)],
        compiler_params=pltpu.CompilerParams(vmem_limit_bytes=SMALL),
    )(rows_of(tgt_weight))


def transfer_kernel(cones, late_from, t_ref, x_ref, tid, live, o_ref, late, late_count, x_scr, o_scr):
    low = low_lanes()
    rows = CHUNKS * cones

    def one(i, carry):
        for u in range(2):
            at = 2 * i + u
            x_scr[u * rows:(u + 1) * rows, :] = x_ref[at].astype(f32)
            for k in range(cones):
                x = x_scr[every(u * rows + k, H, cones), :].astype(bf16)
                o_scr[every(u * rows + k, H, cones), :] = left_product(t_ref[at * cones + k], x, low)
            o_ref[at] = o_scr[u * rows:(u + 1) * rows, :].astype(bf16)
        return carry

    lax.fori_loop(0, x_ref.shape[0] // 2, one, 0, unroll=2)
    slots = tid.shape[0]

    def note(n, count):
        late[count] = n
        return count + jnp.where((tid[n] >= late_from) & (n < live[0]), 1, 0)

    count = lax.fori_loop(0, slots, note, 0, unroll=8)
    late_count[0] = count

    def pad(n, carry):
        late[count + n] = slots
        return carry

    lax.fori_loop(0, LATE_GROUP, pad, 0)


def transfer(t_dense, tgt_transfer, tid, live, late_from):
    cones = tgt_transfer.shape[1]
    rows = rows_of(tgt_transfer)
    slots = tid.shape[0]
    out, late, count = pl.pallas_call(
        functools.partial(transfer_kernel, cones, late_from),
        in_specs=[WHOLE, WHOLE, SCALARS, SCALARS],
        out_specs=[WHOLE, SCALARS, SCALARS],
        out_shape=[
            jax.ShapeDtypeStruct(rows.shape, bf16),
            jax.ShapeDtypeStruct((slots + LATE_GROUP,), jnp.int32),
            jax.ShapeDtypeStruct((1,), jnp.int32),
        ],
        scratch_shapes=[pltpu.VMEM((2 * CHUNKS * cones, LANES), f32)] * 2,
        compiler_params=pltpu.CompilerParams(vmem_limit_bytes=24 * 2**20),
        cost_estimate=pl.CostEstimate(flops=2 * rows.size * W, bytes_accessed=12 * rows.size, transcendentals=0),
    )(t_dense, rows, tid, live)
    return rows_back(out, cones), late, count


def load_table(parts, table, sem):
    copies, at = [], 0
    for part in parts:
        copies.append(pltpu.make_async_copy(part, table.at[pl.ds(at, part.shape[0])], sem.at[len(copies)]))
        at += part.shape[0]
    return copies


def for_each(count, act):
    def one(at, carry):
        act(at)
        return carry

    lax.fori_loop(0, count, one, 0)


def left_kernel(n_parts, block, late_from, tid, live, c_ref, *refs):
    parts = refs[:n_parts]
    o_ref, table, c_all, scr, sem, c_sem = refs[n_parts:]
    step_at, steps = pl.program_id(0), pl.num_programs(0)
    first = step_at * block
    low = low_lanes()
    rows = block * CHUNKS

    def block_copy(at):
        piece = pl.ds(pl.multiple_of(at * rows, rows), rows)
        return pltpu.make_async_copy(c_ref.at[piece], c_all.at[piece], c_sem.at[at])

    @pl.when(step_at == 0)
    def _():
        copies = load_table(parts, table, sem)
        for copy in copies:
            copy.start()
        for_each(steps, lambda at: block_copy(at).start())
        for copy in copies:
            copy.wait()

    block_copy(step_at).wait()

    def step(i, carry):
        i0 = pl.multiple_of(i * GROUP, GROUP)
        n0 = first + i0
        base = pl.multiple_of(n0 * CHUNKS, GROUP * CHUNKS)
        for u in range(GROUP // 8):
            for c in range(0, CHUNKS, 2):
                x = c_all[pl.ds(base + (u * CHUNKS + c) * 8, 16), :].astype(f32)
                scr[pl.ds(u * 8 * PITCH + c, 8, stride=PITCH), :] = x[:8]
                scr[pl.ds(u * 8 * PITCH + c + 1, 8, stride=PITCH), :] = x[8:]
        for n in range(GROUP):
            c = scr[n * PITCH:n * PITCH + H, :].astype(bf16)
            t = tid[n0 + n]
            product = left_product(table[jnp.minimum(t, late_from - 1)], c, low).astype(bf16)
            o_ref[i0 + n] = jnp.where(t < late_from, product, c)
        return carry

    @pl.when(first < live[0])
    def _():
        lax.fori_loop(0, block // GROUP, step, 0, unroll=8)


def left(coupling, tid, live, parts, late_from):
    slots = coupling.shape[0]
    block = 128
    entries = sum(p.shape[0] for p in parts)
    return pl.pallas_call(
        functools.partial(left_kernel, len(parts), block, late_from),
        grid_spec=pltpu.PrefetchScalarGridSpec(
            num_scalar_prefetch=2,
            grid=(slots // block,),
            in_specs=[IN_HBM] + [ANYWHERE] * len(parts),
            out_specs=pl.BlockSpec((block, H, LANES), lambda g, *_: (g, 0, 0)),
            scratch_shapes=[
                pltpu.VMEM((entries, H, LANES), bf16),
                pltpu.VMEM((slots * CHUNKS, LANES), bf16),
                pltpu.VMEM((GROUP * PITCH, LANES), f32),
                pltpu.SemaphoreType.DMA((len(parts),)),
                pltpu.SemaphoreType.DMA((slots // block,)),
            ],
        ),
        out_shape=jax.ShapeDtypeStruct((slots, H, LANES), bf16),
        compiler_params=pltpu.CompilerParams(vmem_limit_bytes=44 * 2**20),
        cost_estimate=pl.CostEstimate(
            flops=8 * coupling.size * W, bytes_accessed=8 * coupling.size, transcendentals=0
        ),
    )(tid, live, slot_rows(coupling), *parts)


def right_kernel(
    n_late, n_parts, chips, block, late_from, tid, sid, live, late, late_count, chip, left_ref, *refs
):
    late_parts, parts = refs[:n_late], refs[n_late:n_late + n_parts]
    o_ref, left_all, late_table, table, out_all, scr = refs[n_late + n_parts:-4]
    sem, late_sem, l_sem, o_sem = refs[-4:]
    low = low_lanes()
    slots = tid.shape[0]
    rows = block * CHUNKS
    blocks = (live[0] + block - 1) // block

    def left_copy(at):
        piece = pl.ds(pl.multiple_of(at * block, block), block)
        return pltpu.make_async_copy(left_ref.at[piece], left_all.at[piece], l_sem.at[at])

    def out_copy(at):
        piece = pl.ds(pl.multiple_of(at * rows, rows), rows)
        return pltpu.make_async_copy(out_all.at[piece], o_ref.at[piece], o_sem.at[at])

    def here(at):
        far = at // 2 + 2 - chips
        there = jnp.where(chip[0] % 2 == 0, chip[0] + far, chip[0] - far)
        return (there >= 0) & (there < chips)

    last = load_table(late_parts, late_table, late_sem)
    columns = load_table(parts, table, sem)
    for copy in last:
        copy.start()
    for_each(blocks, lambda at: left_copy(at).start())
    for at, copy in enumerate(columns):
        pl.when(here(at))(copy.start)

    def clear(at):
        at = blocks + at
        out_all[pl.ds(pl.multiple_of(at * rows, rows), rows), :] = jnp.zeros((rows, LANES), bf16)
        out_copy(at).start()

    for_each(slots // block - blocks, clear)
    for copy in last:
        copy.wait()
    for_each(blocks, lambda at: left_copy(at).wait())

    if n_late:
        def fill(i):
            which = [late[i * LATE_GROUP + n] for n in range(LATE_GROUP)]
            held = [left_all[w] for w in which]
            done = []
            for w, c in zip(which, held):
                t = jnp.maximum(tid[jnp.minimum(w, slots - 1)] - late_from, 0)
                done.append(left_product(late_table[t], c, low).astype(bf16))
            for w, product in zip(which, done):
                left_all[w] = product

        for_each((late_count[0] + LATE_GROUP - 1) // LATE_GROUP, fill)
    for at, copy in enumerate(columns):
        pl.when(here(at))(copy.wait)

    def step(i, carry):
        n0 = pl.multiple_of(i * GROUP, GROUP)
        for n in range(GROUP):
            scr[n * PITCH:n * PITCH + H, :] = right_product(left_all[n0 + n], table[sid[n0 + n]], low)
        keep = lax.broadcasted_iota(jnp.int32, (8, LANES), 0) + n0
        base = pl.multiple_of(n0 * CHUNKS, GROUP * CHUNKS)
        for u in range(GROUP // 8):
            mask = keep + u * 8 < live[0]
            for c in range(0, CHUNKS, 2):
                pair = [
                    jnp.where(mask, scr[pl.ds(u * 8 * PITCH + c + e, 8, stride=PITCH), :], 0.0)
                    for e in range(2)
                ]
                out_all[pl.ds(base + (u * CHUNKS + c) * 8, 16), :] = jnp.concatenate(pair, axis=0).astype(bf16)
        return carry

    per = block // GROUP

    def work(at):
        lax.fori_loop(0, per, lambda i, carry: step(at * per + i, carry), 0, unroll=12)
        out_copy(at).start()

    for_each(blocks, work)
    for_each(slots // block, lambda at: out_copy(at).wait())


def right(left_all, tid, sid, live, late, late_count, chip, late_parts, parts, late_from, chips):
    slots = left_all.shape[0]
    block = 192 if slots % 128 == 0 else GROUP
    n_late, entries = sum(p.shape[0] for p in late_parts), sum(p.shape[0] for p in parts)
    rows = pl.pallas_call(
        functools.partial(right_kernel, len(late_parts), len(parts), chips, block, late_from),
        in_specs=[SCALARS] * 6 + [ANYWHERE] * (1 + len(late_parts) + len(parts)),
        out_specs=ANYWHERE,
        scratch_shapes=[
            pltpu.VMEM((slots + 1, H, LANES), bf16),
            pltpu.VMEM((max(n_late, 8), H, LANES), bf16),
            pltpu.VMEM((entries, H, LANES), bf16),
            pltpu.VMEM((slots * CHUNKS, LANES), bf16),
            pltpu.VMEM((GROUP * PITCH, LANES), f32),
            pltpu.SemaphoreType.DMA((len(parts),)),
            pltpu.SemaphoreType.DMA((max(len(late_parts), 1),)),
            pltpu.SemaphoreType.DMA((slots // block,)),
            pltpu.SemaphoreType.DMA((slots // block,)),
        ],
        out_shape=jax.ShapeDtypeStruct((slots * CHUNKS, LANES), bf16),
        compiler_params=pltpu.CompilerParams(vmem_limit_bytes=30 * 2**20),
    )(tid, sid, live, late, late_count, chip, left_all, *late_parts, *parts)
    return slot_rows_back(rows)


def square_pairs(rows):
    near, far = [], []
    for row in range(rows):
        for at in range(4):
            near.append((row * 4 + at, row * 4 + (at ^ (1 + row % 2))))
            far.append((row * 4 + at, row * 4 + (at ^ (2 - row % 2))))
    return near, far


def pass_on(part, pairs):
    return lax.ppermute(part, ("tgt", "src"), pairs)


def column_pairs(chips):
    def far(z):
        return z if z in (0, chips - 1) else ((z - 1) ^ 1) + 1

    near_pairs = [(2 * z + c, 2 * (z ^ 1) + c) for z in range(chips) for c in range(2)]
    far_pairs = [(2 * z + c, 2 * far(z) + c) for z in range(chips) for c in range(2)]
    return near_pairs, far_pairs, [(i, i ^ 1) for i in range(2 * chips)]


def send(part, pairs):
    return lax.ppermute(part, "tgt", pairs)


def slot_tables(n_src, chips, row, col, t_shape, s_shape, block_tgt, block_src, block_cone):
    t_clu, t_cones = t_shape
    s_clu, s_cones = s_shape
    tloc = jnp.clip(block_tgt - row * t_clu, 0, t_clu - 1)
    sloc = jnp.clip(block_src - col * s_clu, 0, s_clu - 1)
    owner = block_cone // t_cones
    if n_src == 4:
        part = owner ^ col
        part = jnp.where((part % 3 != 0) & (row % 2 == 1), 3 - part, part)
        tid = (part * t_clu + tloc) * t_cones + block_cone % t_cones
        late_from = 3 * t_clu * t_cones
    else:
        tid = (owner * t_clu + tloc) * t_cones + block_cone % t_cones
        late_from = n_src * t_clu * t_cones
    owner = block_cone // s_cones
    z = row // 2
    ahead = (owner // 2 - z) * (1 - 2 * (z % 2))
    part = (ahead + chips - 2) * 2 + ((owner ^ row) & 1)
    return tid, late_from, (part * s_clu + sloc) * s_cones + block_cone % s_cones


def local(n_src, chips, tgt_weight, src_weight, coupling, block_tgt, block_src, block_cone, block_count, tgt_transfer):
    row, col = lax.axis_index("tgt"), lax.axis_index("src")
    near, far, cores = column_pairs(chips)
    fence = lax.optimization_barrier
    square = n_src == 4
    t_shape, s_shape = tgt_weight.shape[:2], src_weight.shape[:2]

    s_dense = prep_src(src_weight)
    a, b = send(s_dense, near), send(s_dense, far)
    t_dense = prep_tgt(tgt_weight)
    kept, t_dense = fence((s_dense, t_dense))
    own = [s_dense, send(kept, cores)]
    slots = (block_tgt, block_src, block_cone)
    a, b, own, tgt_transfer, slots = fence((a, b, own, tgt_transfer, slots))
    if square:
        one, other = square_pairs(2 * chips)
        p, q = pass_on(t_dense, one), pass_on(t_dense, other)
    else:
        gathered = lax.all_gather(t_dense, "src", axis=0).reshape(-1, H, LANES)

    tid, late_from, sid = slot_tables(n_src, chips, row, col, t_shape, s_shape, *slots)
    new_transfer, late, late_count = transfer(t_dense, tgt_transfer, tid, block_count, late_from)
    ahead_parts, behind_parts = [], []
    for step in range(2, chips):
        kept_a = a
        kept_b, late = fence((b, late)) if step == 2 else (b, late)
        a, b = send(b, near), send(a, far) if step < chips - 1 else None
        if step == 3 and square:
            kept_a, kept_b = kept_x, kept_y
        ahead_parts.append([kept_a, send(kept_a, cores)])
        behind_parts.append([kept_b, send(kept_b, cores)])
        if step == 2 and square:
            a, b, late = fence((a, b, late))
            p, q, late, sid, kept_x, kept_y, ahead_parts = fence((p, q, late, sid, a, b, ahead_parts))
            d = pass_on(p, other)

    t_parts, late_parts = ([t_dense, p, q], [d]) if square else ([gathered], [])
    left_all = left(coupling, tid, block_count, t_parts, late_from)
    a, left_all = fence((a, left_all))
    ahead_parts.append([a, send(a, cores)])
    s_parts = sum(behind_parts[::-1] + [own] + ahead_parts, [])
    chip = (row // 2).reshape(1)
    new_coupling = right(
        left_all, tid, sid, block_count, late, late_count, chip, late_parts, s_parts, late_from, chips
    )
    return new_coupling, new_transfer


def solution(mesh):
    n_src, chips = mesh.shape["src"], mesh.shape["tgt"] // 2
    both = ("tgt", "src")
    return jax.shard_map(
        functools.partial(local, n_src, chips),
        mesh=mesh,
        in_specs=(
            P("tgt", "src", None),
            P("src", "tgt", None),
            P(both, None),
            P(both),
            P(both),
            P(both),
            P(both),
            P("tgt", "src", None),
        ),
        out_specs=(P(both, None), P("tgt", "src", None)),
        check_vma=False,
    )
```

```python
import functools

import jax
import jax.numpy as jnp
from jax import lax
from jax.experimental import pallas as pl
from jax.experimental.pallas import tpu as pltpu
from jax.sharding import PartitionSpec as P

W = 64
WW = 4096
CONES = 16
H = W // 2
LANES = 2 * W
CHUNKS = WW // LANES
SPARE = 2 * H
PITCH = H + 1
GROUP = 16
f32, bf16 = jnp.float32, jnp.bfloat16
LATE_GROUP = 64
SMALL, LARGE = 12 * 2**20, 60 * 2**20


def swap_halves(x):
    return jnp.concatenate([x[:, W:], x[:, :W]], axis=1)


def low_lanes():
    return lax.broadcasted_iota(jnp.int32, (H, LANES), 1) < W


def left_product(t, c, low):
    lhs = jnp.concatenate([t[:, :W], t[:, W:]], axis=0)
    rhs = jnp.concatenate([c, swap_halves(c)], axis=0)
    y = jnp.dot(lhs, rhs, preferred_element_type=f32)
    return jnp.where(low, y[:H], y[H:])


def right_product(left, s, low):
    lhs = jnp.concatenate([left[:, :W], left[:, W:]], axis=0).astype(bf16)
    turned = swap_halves(s)
    rhs = jnp.concatenate([jnp.where(low, s, turned), jnp.where(low, turned, s)], axis=0)
    y = jnp.dot(lhs, rhs, preferred_element_type=f32)
    return jnp.where(low, y[:H], y[H:])


def rows_of(array):
    n, cones, _ = array.shape
    return array.reshape(n, cones, CHUNKS, LANES).transpose(0, 2, 1, 3).reshape(n, CHUNKS * cones, LANES)


def rows_back(rows, cones):
    n = rows.shape[0]
    return rows.reshape(n, CHUNKS, cones, LANES).transpose(0, 2, 1, 3).reshape(n, cones, WW)


def slot_rows(array):
    n = array.shape[0]
    return array.reshape(n // 8, 8, CHUNKS, LANES).transpose(0, 2, 1, 3).reshape(n * CHUNKS, LANES)


def slot_rows_back(rows):
    n = rows.shape[0] // CHUNKS
    return rows.reshape(n // 8, CHUNKS, 8, LANES).transpose(0, 2, 1, 3).reshape(n, WW)


def every(start, count, pitch):
    return pl.ds(start, count) if pitch == 1 else pl.ds(start, count, stride=pitch)


WHOLE = pl.BlockSpec(memory_space=pltpu.VMEM)
ANYWHERE = pl.BlockSpec(memory_space=pl.ANY)
IN_HBM = pl.BlockSpec(memory_space=pltpu.HBM)
SCALARS = pl.BlockSpec(memory_space=pltpu.SMEM)


def prep_src_kernel(cones, s_ref, s_out, scr):
    row = lax.broadcasted_iota(jnp.int32, (LANES, 4 * LANES), 0)
    lane = lax.broadcasted_iota(jnp.int32, (LANES, 4 * LANES), 1)
    same = (row // H) == (lane // LANES)
    even = jnp.where(same & (lane % W == 2 * (row % H)), 1.0, 0.0).astype(bf16)
    odd = jnp.where(same & (lane % W == 2 * (row % H) + 1), 1.0, 0.0).astype(bf16)
    low = low_lanes()
    rows = CHUNKS * cones
    clusters = 8 // cones

    def turn(i, carry):
        for u in range(clusters):
            scr[u * rows:(u + 1) * rows, :] = s_ref[i * clusters + u].astype(f32)
        blocks = [scr[every(u * rows + k, H, cones), :] for u in range(clusters) for k in range(cones)]
        for half in range(2):
            up = jnp.concatenate(blocks[4 * half:4 * half + 4], axis=0).T.astype(bf16)
            both = jnp.dot(up[:W], even, preferred_element_type=f32) + jnp.dot(
                up[W:], odd, preferred_element_type=f32
            )
            for m in range(4):
                d = both[:, m * LANES:(m + 1) * LANES]
                s_out[i * 8 + 4 * half + m] = jnp.where(low, d[:H], d[H:]).astype(bf16)
        return carry

    lax.fori_loop(0, s_out.shape[0] // 8, turn, 0, unroll=2)


def prep_src(src_weight):
    n, cones = src_weight.shape[0], src_weight.shape[1]
    return pl.pallas_call(
        functools.partial(prep_src_kernel, cones),
        in_specs=[WHOLE],
        out_specs=WHOLE,
        out_shape=jax.ShapeDtypeStruct((n * cones, H, LANES), bf16),
        scratch_shapes=[pltpu.VMEM((8 * H + SPARE, LANES), f32)],
        compiler_params=pltpu.CompilerParams(vmem_limit_bytes=SMALL),
    )(rows_of(src_weight))


def prep_tgt_kernel(cones, t_ref, out, scr):
    row = lax.broadcasted_iota(jnp.int32, (LANES, LANES), 0)
    lane = lax.broadcasted_iota(jnp.int32, (LANES, LANES), 1)
    g, at = lane // W, lane % W
    odd_col = (at // H) ^ g
    order = jnp.where(row == g * W + 2 * (at % H) + odd_col, 1.0, 0.0).astype(bf16)
    rows = CHUNKS * cones

    def sort(i, carry):
        for u in range(2):
            at = 2 * i + u
            scr[u * rows:(u + 1) * rows, :] = jnp.dot(t_ref[at], order, preferred_element_type=f32)
            for k in range(cones):
                out[at * cones + k] = scr[every(u * rows + k, H, cones), :].astype(bf16)
        return carry

    lax.fori_loop(0, t_ref.shape[0] // 2, sort, 0, unroll=2)


def prep_tgt(tgt_weight):
    n, cones = tgt_weight.shape[0], tgt_weight.shape[1]
    return pl.pallas_call(
        functools.partial(prep_tgt_kernel, cones),
        in_specs=[WHOLE],
        out_specs=WHOLE,
        out_shape=jax.ShapeDtypeStruct((n * cones, H, LANES), bf16),
        scratch_shapes=[pltpu.VMEM((2 * CHUNKS * cones + SPARE, LANES), f32)],
        compiler_params=pltpu.CompilerParams(vmem_limit_bytes=SMALL),
    )(rows_of(tgt_weight))


def transfer_kernel(cones, late_from, t_ref, x_ref, tid, live, o_ref, late, late_count, x_scr, o_scr):
    low = low_lanes()
    rows = CHUNKS * cones

    def one(i, carry):
        for u in range(2):
            at = 2 * i + u
            x_scr[u * rows:(u + 1) * rows, :] = x_ref[at].astype(f32)
            for k in range(cones):
                x = x_scr[every(u * rows + k, H, cones), :].astype(bf16)
                o_scr[every(u * rows + k, H, cones), :] = left_product(t_ref[at * cones + k], x, low)
            o_ref[at] = o_scr[u * rows:(u + 1) * rows, :].astype(bf16)
        return carry

    lax.fori_loop(0, x_ref.shape[0] // 2, one, 0, unroll=2)
    slots = tid.shape[0]

    def note(n, count):
        late[count] = n
        return count + jnp.where((tid[n] >= late_from) & (n < live[0]), 1, 0)

    count = lax.fori_loop(0, slots, note, 0, unroll=8)
    late_count[0] = count

    def pad(n, carry):
        late[count + n] = slots
        return carry

    lax.fori_loop(0, LATE_GROUP, pad, 0)


def transfer(t_dense, tgt_transfer, tid, live, late_from):
    cones = tgt_transfer.shape[1]
    rows = rows_of(tgt_transfer)
    slots = tid.shape[0]
    out, late, count = pl.pallas_call(
        functools.partial(transfer_kernel, cones, late_from),
        in_specs=[WHOLE, WHOLE, SCALARS, SCALARS],
        out_specs=[WHOLE, SCALARS, SCALARS],
        out_shape=[
            jax.ShapeDtypeStruct(rows.shape, bf16),
            jax.ShapeDtypeStruct((slots + LATE_GROUP,), jnp.int32),
            jax.ShapeDtypeStruct((1,), jnp.int32),
        ],
        scratch_shapes=[pltpu.VMEM((2 * CHUNKS * cones + SPARE, LANES), f32)] * 2,
        compiler_params=pltpu.CompilerParams(vmem_limit_bytes=24 * 2**20),
        cost_estimate=pl.CostEstimate(flops=2 * rows.size * W, bytes_accessed=12 * rows.size, transcendentals=0),
    )(t_dense, rows, tid, live)
    return rows_back(out, cones), late, count


def load_table(parts, table, sem):
    copies, at = [], 0
    for part in parts:
        copies.append(pltpu.make_async_copy(part, table.at[pl.ds(at, part.shape[0])], sem.at[len(copies)]))
        at += part.shape[0]
    return copies


def for_each(count, act):
    def one(at, carry):
        act(at)
        return carry

    lax.fori_loop(0, count, one, 0)


def left_kernel(n_parts, block, late_from, tid, live, c_ref, *refs):
    parts = refs[:n_parts]
    o_ref, table, c_all, scr, sem, c_sem = refs[n_parts:]
    step_at, steps = pl.program_id(0), pl.num_programs(0)
    first = step_at * block
    low = low_lanes()
    rows = block * CHUNKS

    def block_copy(at):
        piece = pl.ds(pl.multiple_of(at * rows, rows), rows)
        return pltpu.make_async_copy(c_ref.at[piece], c_all.at[piece], c_sem.at[at])

    @pl.when(step_at == 0)
    def _():
        copies = load_table(parts, table, sem)
        for copy in copies:
            copy.start()
        for_each(steps, lambda at: block_copy(at).start())
        for copy in copies:
            copy.wait()

    block_copy(step_at).wait()

    def step(i, carry):
        i0 = pl.multiple_of(i * GROUP, GROUP)
        n0 = first + i0
        base = pl.multiple_of(n0 * CHUNKS, GROUP * CHUNKS)
        for u in range(GROUP // 8):
            for c in range(0, CHUNKS, 2):
                x = c_all[pl.ds(base + (u * CHUNKS + c) * 8, 16), :].astype(f32)
                scr[pl.ds(u * 8 * PITCH + c, 8, stride=PITCH), :] = x[:8]
                scr[pl.ds(u * 8 * PITCH + c + 1, 8, stride=PITCH), :] = x[8:]
        for n in range(GROUP):
            c = scr[n * PITCH:n * PITCH + H, :].astype(bf16)
            t = tid[n0 + n]
            product = left_product(table[jnp.minimum(t, late_from - 1)], c, low).astype(bf16)
            o_ref[i0 + n] = jnp.where(t < late_from, product, c)
        return carry

    @pl.when(first < live[0])
    def _():
        lax.fori_loop(0, block // GROUP, step, 0, unroll=8)


def left(coupling, tid, live, parts, late_from):
    slots = coupling.shape[0]
    block = 128
    entries = sum(p.shape[0] for p in parts)
    return pl.pallas_call(
        functools.partial(left_kernel, len(parts), block, late_from),
        grid_spec=pltpu.PrefetchScalarGridSpec(
            num_scalar_prefetch=2,
            grid=(slots // block,),
            in_specs=[IN_HBM] + [ANYWHERE] * len(parts),
            out_specs=pl.BlockSpec((block, H, LANES), lambda g, *_: (g, 0, 0)),
            scratch_shapes=[
                pltpu.VMEM((entries, H, LANES), bf16),
                pltpu.VMEM((slots * CHUNKS, LANES), bf16),
                pltpu.VMEM((GROUP * PITCH + SPARE, LANES), f32),
                pltpu.SemaphoreType.DMA((len(parts),)),
                pltpu.SemaphoreType.DMA((slots // block,)),
            ],
        ),
        out_shape=jax.ShapeDtypeStruct((slots, H, LANES), bf16),
        compiler_params=pltpu.CompilerParams(vmem_limit_bytes=44 * 2**20),
        cost_estimate=pl.CostEstimate(
            flops=8 * coupling.size * W, bytes_accessed=8 * coupling.size, transcendentals=0
        ),
    )(tid, live, slot_rows(coupling), *parts)


def right_kernel(
    n_late, n_parts, chips, block, late_from, tid, sid, live, late, late_count, chip, left_ref, *refs
):
    late_parts, parts = refs[:n_late], refs[n_late:n_late + n_parts]
    o_ref, left_all, late_table, table, out_all, scr = refs[n_late + n_parts:-4]
    sem, late_sem, l_sem, o_sem = refs[-4:]
    low = low_lanes()
    slots = tid.shape[0]
    rows = block * CHUNKS
    blocks = (live[0] + block - 1) // block

    def left_copy(at):
        piece = pl.ds(pl.multiple_of(at * block, block), block)
        return pltpu.make_async_copy(left_ref.at[piece], left_all.at[piece], l_sem.at[at])

    def out_copy(at):
        piece = pl.ds(pl.multiple_of(at * rows, rows), rows)
        return pltpu.make_async_copy(out_all.at[piece], o_ref.at[piece], o_sem.at[at])

    def here(at):
        far = at // 2 + 2 - chips
        there = jnp.where(chip[0] % 2 == 0, chip[0] + far, chip[0] - far)
        return (there >= 0) & (there < chips)

    last = load_table(late_parts, late_table, late_sem)
    columns = load_table(parts, table, sem)
    for copy in last:
        copy.start()
    for_each(blocks, lambda at: left_copy(at).start())
    for at, copy in enumerate(columns):
        pl.when(here(at))(copy.start)

    def clear(at):
        at = blocks + at
        out_all[pl.ds(pl.multiple_of(at * rows, rows), rows), :] = jnp.zeros((rows, LANES), bf16)
        out_copy(at).start()

    for_each(slots // block - blocks, clear)
    for copy in last:
        copy.wait()
    for_each(blocks, lambda at: left_copy(at).wait())

    if n_late:
        def fill(i):
            which = [late[i * LATE_GROUP + n] for n in range(LATE_GROUP)]
            held = [left_all[w] for w in which]
            done = []
            for w, c in zip(which, held):
                t = jnp.maximum(tid[jnp.minimum(w, slots - 1)] - late_from, 0)
                done.append(left_product(late_table[t], c, low).astype(bf16))
            for w, product in zip(which, done):
                left_all[w] = product

        for_each((late_count[0] + LATE_GROUP - 1) // LATE_GROUP, fill)
    for at, copy in enumerate(columns):
        pl.when(here(at))(copy.wait)

    def step(i, carry):
        n0 = pl.multiple_of(i * GROUP, GROUP)
        for n in range(GROUP):
            scr[n * PITCH:n * PITCH + H, :] = right_product(left_all[n0 + n], table[sid[n0 + n]], low)
        keep = lax.broadcasted_iota(jnp.int32, (8, LANES), 0) + n0
        base = pl.multiple_of(n0 * CHUNKS, GROUP * CHUNKS)
        for u in range(GROUP // 8):
            mask = keep + u * 8 < live[0]
            for c in range(0, CHUNKS, 2):
                pair = [
                    jnp.where(mask, scr[pl.ds(u * 8 * PITCH + c + e, 8, stride=PITCH), :], 0.0)
                    for e in range(2)
                ]
                out_all[pl.ds(base + (u * CHUNKS + c) * 8, 16), :] = jnp.concatenate(pair, axis=0).astype(bf16)
        return carry

    per = block // GROUP

    def work(at):
        lax.fori_loop(0, per, lambda i, carry: step(at * per + i, carry), 0, unroll=12)
        out_copy(at).start()

    for_each(blocks, work)
    for_each(slots // block, lambda at: out_copy(at).wait())


def right(left_all, tid, sid, live, late, late_count, chip, late_parts, parts, late_from, chips):
    slots = left_all.shape[0]
    block = 192 if slots % 128 == 0 else GROUP
    n_late, entries = sum(p.shape[0] for p in late_parts), sum(p.shape[0] for p in parts)
    rows = pl.pallas_call(
        functools.partial(right_kernel, len(late_parts), len(parts), chips, block, late_from),
        in_specs=[SCALARS] * 6 + [ANYWHERE] * (1 + len(late_parts) + len(parts)),
        out_specs=ANYWHERE,
        scratch_shapes=[
            pltpu.VMEM((slots + 1, H, LANES), bf16),
            pltpu.VMEM((max(n_late, 8), H, LANES), bf16),
            pltpu.VMEM((entries, H, LANES), bf16),
            pltpu.VMEM((slots * CHUNKS, LANES), bf16),
            pltpu.VMEM((GROUP * PITCH + SPARE, LANES), f32),
            pltpu.SemaphoreType.DMA((len(parts),)),
            pltpu.SemaphoreType.DMA((max(len(late_parts), 1),)),
            pltpu.SemaphoreType.DMA((slots // block,)),
            pltpu.SemaphoreType.DMA((slots // block,)),
        ],
        out_shape=jax.ShapeDtypeStruct((slots * CHUNKS, LANES), bf16),
        compiler_params=pltpu.CompilerParams(vmem_limit_bytes=30 * 2**20),
    )(tid, sid, live, late, late_count, chip, left_all, *late_parts, *parts)
    return slot_rows_back(rows)


def square_pairs(rows):
    near, far = [], []
    for row in range(rows):
        for at in range(4):
            near.append((row * 4 + at, row * 4 + (at ^ (1 + row % 2))))
            far.append((row * 4 + at, row * 4 + (at ^ (2 - row % 2))))
    return near, far


def pass_on(part, pairs):
    return lax.ppermute(part, ("tgt", "src"), pairs)


def column_pairs(chips):
    def far(z):
        return z if z in (0, chips - 1) else ((z - 1) ^ 1) + 1

    near_pairs = [(2 * z + c, 2 * (z ^ 1) + c) for z in range(chips) for c in range(2)]
    far_pairs = [(2 * z + c, 2 * far(z) + c) for z in range(chips) for c in range(2)]
    return near_pairs, far_pairs, [(i, i ^ 1) for i in range(2 * chips)]


def send(part, pairs):
    return lax.ppermute(part, "tgt", pairs)


def slot_tables(n_src, chips, row, col, t_shape, s_shape, block_tgt, block_src, block_cone):
    t_clu, t_cones = t_shape
    s_clu, s_cones = s_shape
    tloc = jnp.clip(block_tgt - row * t_clu, 0, t_clu - 1)
    sloc = jnp.clip(block_src - col * s_clu, 0, s_clu - 1)
    owner = block_cone // t_cones
    if n_src == 4:
        part = owner ^ col
        part = jnp.where((part % 3 != 0) & (row % 2 == 1), 3 - part, part)
        tid = (part * t_clu + tloc) * t_cones + block_cone % t_cones
        late_from = 3 * t_clu * t_cones
    else:
        tid = (owner * t_clu + tloc) * t_cones + block_cone % t_cones
        late_from = n_src * t_clu * t_cones
    owner = block_cone // s_cones
    z = row // 2
    ahead = (owner // 2 - z) * (1 - 2 * (z % 2))
    part = (ahead + chips - 2) * 2 + ((owner ^ row) & 1)
    return tid, late_from, (part * s_clu + sloc) * s_cones + block_cone % s_cones


def local(n_src, chips, tgt_weight, src_weight, coupling, block_tgt, block_src, block_cone, block_count, tgt_transfer):
    row, col = lax.axis_index("tgt"), lax.axis_index("src")
    near, far, cores = column_pairs(chips)
    fence = lax.optimization_barrier
    square = n_src == 4
    t_shape, s_shape = tgt_weight.shape[:2], src_weight.shape[:2]

    s_dense = prep_src(src_weight)
    a, b = send(s_dense, near), send(s_dense, far)
    t_dense = prep_tgt(tgt_weight)
    kept, t_dense = fence((s_dense, t_dense))
    own = [s_dense, send(kept, cores)]
    slots = (block_tgt, block_src, block_cone)
    a, b, own, tgt_transfer, slots = fence((a, b, own, tgt_transfer, slots))
    if square:
        one, other = square_pairs(2 * chips)
        p, q = pass_on(t_dense, one), pass_on(t_dense, other)
    else:
        gathered = lax.all_gather(t_dense, "src", axis=0).reshape(-1, H, LANES)

    tid, late_from, sid = slot_tables(n_src, chips, row, col, t_shape, s_shape, *slots)
    new_transfer, late, late_count = transfer(t_dense, tgt_transfer, tid, block_count, late_from)
    ahead_parts, behind_parts = [], []
    for step in range(2, chips):
        kept_a = a
        kept_b, late = fence((b, late)) if step == 2 else (b, late)
        a, b = send(b, near), send(a, far) if step < chips - 1 else None
        if step == 3 and square:
            kept_a, kept_b = kept_x, kept_y
        ahead_parts.append([kept_a, send(kept_a, cores)])
        behind_parts.append([kept_b, send(kept_b, cores)])
        if step == 2 and square:
            a, b, late = fence((a, b, late))
            p, q, late, sid, kept_x, kept_y, ahead_parts = fence((p, q, late, sid, a, b, ahead_parts))
            d = pass_on(p, other)

    t_parts, late_parts = ([t_dense, p, q], [d]) if square else ([gathered], [])
    left_all = left(coupling, tid, block_count, t_parts, late_from)
    a, left_all = fence((a, left_all))
    ahead_parts.append([a, send(a, cores)])
    s_parts = sum(behind_parts[::-1] + [own] + ahead_parts, [])
    chip = (row // 2).reshape(1)
    new_coupling = right(
        left_all, tid, sid, block_count, late, late_count, chip, late_parts, s_parts, late_from, chips
    )
    return new_coupling, new_transfer


def solution(mesh):
    n_src, chips = mesh.shape["src"], mesh.shape["tgt"] // 2
    both = ("tgt", "src")
    return jax.shard_map(
        functools.partial(local, n_src, chips),
        mesh=mesh,
        in_specs=(
            P("tgt", "src", None),
            P("src", "tgt", None),
            P(both, None),
            P(both),
            P(both),
            P(both),
            P(both),
            P("tgt", "src", None),
        ),
        out_specs=(P(both, None), P("tgt", "src", None)),
        check_vma=False,
    )
```

```python
import functools

import jax
import jax.numpy as jnp
from jax import lax
from jax.experimental import pallas as pl
from jax.experimental.pallas import tpu as pltpu
from jax.sharding import PartitionSpec as P

W = 64
WW = 4096
CONES = 16
H = W // 2
LANES = 2 * W
CHUNKS = WW // LANES
SPARE = 2 * H
PITCH = H + 1
GROUP = 16
f32, bf16 = jnp.float32, jnp.bfloat16
LATE_GROUP = 64
SMALL, LARGE = 12 * 2**20, 60 * 2**20


def swap_halves(x):
    return jnp.concatenate([x[:, W:], x[:, :W]], axis=1)


def low_lanes():
    return lax.broadcasted_iota(jnp.int32, (H, LANES), 1) < W


def left_product(t, c, low):
    lhs = jnp.concatenate([t[:, :W], t[:, W:]], axis=0)
    rhs = jnp.concatenate([c, swap_halves(c)], axis=0)
    y = jnp.dot(lhs, rhs, preferred_element_type=f32)
    return jnp.where(low, y[:H], y[H:])


def right_product(left, s, low):
    lhs = jnp.concatenate([left[:, :W], left[:, W:]], axis=0).astype(bf16)
    turned = swap_halves(s)
    rhs = jnp.concatenate([jnp.where(low, s, turned), jnp.where(low, turned, s)], axis=0)
    y = jnp.dot(lhs, rhs, preferred_element_type=f32)
    return jnp.where(low, y[:H], y[H:])


def rows_of(array):
    n, cones, _ = array.shape
    return array.reshape(n, cones, CHUNKS, LANES).transpose(0, 2, 1, 3).reshape(n, CHUNKS * cones, LANES)


def rows_back(rows, cones):
    n = rows.shape[0]
    return rows.reshape(n, CHUNKS, cones, LANES).transpose(0, 2, 1, 3).reshape(n, cones, WW)


def slot_rows(array):
    n = array.shape[0]
    return array.reshape(n // 8, 8, CHUNKS, LANES).transpose(0, 2, 1, 3).reshape(n * CHUNKS, LANES)


def slot_rows_back(rows):
    n = rows.shape[0] // CHUNKS
    return rows.reshape(n // 8, CHUNKS, 8, LANES).transpose(0, 2, 1, 3).reshape(n, WW)


def every(start, count, pitch):
    return pl.ds(start, count) if pitch == 1 else pl.ds(start, count, stride=pitch)


WHOLE = pl.BlockSpec(memory_space=pltpu.VMEM)
ANYWHERE = pl.BlockSpec(memory_space=pl.ANY)
IN_HBM = pl.BlockSpec(memory_space=pltpu.HBM)
SCALARS = pl.BlockSpec(memory_space=pltpu.SMEM)


def prep_src_kernel(cones, s_ref, s_out, scr):
    row = lax.broadcasted_iota(jnp.int32, (LANES, 4 * LANES), 0)
    lane = lax.broadcasted_iota(jnp.int32, (LANES, 4 * LANES), 1)
    same = (row // H) == (lane // LANES)
    even = jnp.where(same & (lane % W == 2 * (row % H)), 1.0, 0.0).astype(bf16)
    odd = jnp.where(same & (lane % W == 2 * (row % H) + 1), 1.0, 0.0).astype(bf16)
    low = low_lanes()
    rows = CHUNKS * cones
    clusters = 8 // cones

    def turn(i, carry):
        for u in range(clusters):
            scr[u * rows:(u + 1) * rows, :] = s_ref[i * clusters + u].astype(f32)
        blocks = [scr[every(u * rows + k, H, cones), :] for u in range(clusters) for k in range(cones)]
        for half in range(2):
            up = jnp.concatenate(blocks[4 * half:4 * half + 4], axis=0).T.astype(bf16)
            both = jnp.dot(up[:W], even, preferred_element_type=f32) + jnp.dot(
                up[W:], odd, preferred_element_type=f32
            )
            for m in range(4):
                d = both[:, m * LANES:(m + 1) * LANES]
                s_out[i * 8 + 4 * half + m] = jnp.where(low, d[:H], d[H:]).astype(bf16)
        return carry

    lax.fori_loop(0, s_out.shape[0] // 8, turn, 0, unroll=2)


def prep_src(src_weight):
    n, cones = src_weight.shape[0], src_weight.shape[1]
    return pl.pallas_call(
        functools.partial(prep_src_kernel, cones),
        in_specs=[WHOLE],
        out_specs=WHOLE,
        out_shape=jax.ShapeDtypeStruct((n * cones, H, LANES), bf16),
        scratch_shapes=[pltpu.VMEM((8 * H + SPARE, LANES), f32)],
        compiler_params=pltpu.CompilerParams(vmem_limit_bytes=SMALL),
    )(rows_of(src_weight))


def prep_tgt_kernel(cones, t_ref, out, scr):
    row = lax.broadcasted_iota(jnp.int32, (LANES, LANES), 0)
    lane = lax.broadcasted_iota(jnp.int32, (LANES, LANES), 1)
    g, at = lane // W, lane % W
    odd_col = (at // H) ^ g
    order = jnp.where(row == g * W + 2 * (at % H) + odd_col, 1.0, 0.0).astype(bf16)
    rows = CHUNKS * cones

    def sort(i, carry):
        for u in range(2):
            at = 2 * i + u
            scr[u * rows:(u + 1) * rows, :] = jnp.dot(t_ref[at], order, preferred_element_type=f32)
            for k in range(cones):
                out[at * cones + k] = scr[every(u * rows + k, H, cones), :].astype(bf16)
        return carry

    lax.fori_loop(0, t_ref.shape[0] // 2, sort, 0, unroll=2)


def prep_tgt(tgt_weight):
    n, cones = tgt_weight.shape[0], tgt_weight.shape[1]
    return pl.pallas_call(
        functools.partial(prep_tgt_kernel, cones),
        in_specs=[WHOLE],
        out_specs=WHOLE,
        out_shape=jax.ShapeDtypeStruct((n * cones, H, LANES), bf16),
        scratch_shapes=[pltpu.VMEM((2 * CHUNKS * cones + SPARE, LANES), f32)],
        compiler_params=pltpu.CompilerParams(vmem_limit_bytes=SMALL),
    )(rows_of(tgt_weight))


def transfer_kernel(cones, t_ref, x_ref, o_ref, x_scr, o_scr):
    low = low_lanes()
    rows = CHUNKS * cones

    def one(i, carry):
        for u in range(2):
            at = 2 * i + u
            x_scr[u * rows:(u + 1) * rows, :] = x_ref[at].astype(f32)
            for k in range(cones):
                x = x_scr[every(u * rows + k, H, cones), :].astype(bf16)
                o_scr[every(u * rows + k, H, cones), :] = left_product(t_ref[at * cones + k], x, low)
            o_ref[at] = o_scr[u * rows:(u + 1) * rows, :].astype(bf16)
        return carry

    lax.fori_loop(0, x_ref.shape[0] // 2, one, 0, unroll=2)


def transfer(t_dense, tgt_transfer):
    cones = tgt_transfer.shape[1]
    rows = rows_of(tgt_transfer)
    out = pl.pallas_call(
        functools.partial(transfer_kernel, cones),
        in_specs=[WHOLE, WHOLE],
        out_specs=WHOLE,
        out_shape=jax.ShapeDtypeStruct(rows.shape, bf16),
        scratch_shapes=[pltpu.VMEM((2 * CHUNKS * cones + SPARE, LANES), f32)] * 2,
        compiler_params=pltpu.CompilerParams(vmem_limit_bytes=24 * 2**20),
        cost_estimate=pl.CostEstimate(flops=2 * rows.size * W, bytes_accessed=12 * rows.size, transcendentals=0),
    )(t_dense, rows)
    return rows_back(out, cones)


def load_table(parts, table, sem):
    copies, at = [], 0
    for part in parts:
        copies.append(pltpu.make_async_copy(part, table.at[pl.ds(at, part.shape[0])], sem.at[len(copies)]))
        at += part.shape[0]
    return copies


def for_each(count, act):
    def one(at, carry):
        act(at)
        return carry

    lax.fori_loop(0, count, one, 0)


def note_late(late_from, tid, live, late, late_count):
    slots = tid.shape[0]

    def note(n, count):
        late[count] = n
        return count + jnp.where((tid[n] >= late_from) & (n < live[0]), 1, 0)

    count = lax.fori_loop(0, slots, note, 0, unroll=8)
    late_count[0] = count

    def pad(n, carry):
        late[count + n] = slots
        return carry

    lax.fori_loop(0, LATE_GROUP, pad, 0)


def left_kernel(n_parts, block, late_from, tid, live, c_ref, *refs):
    parts = refs[:n_parts]
    o_ref, late, late_count, table, c_all, scr, sem, c_sem = refs[n_parts:]
    step_at, steps = pl.program_id(0), pl.num_programs(0)
    first = step_at * block
    low = low_lanes()
    rows = block * CHUNKS

    def block_copy(at):
        piece = pl.ds(pl.multiple_of(at * rows, rows), rows)
        return pltpu.make_async_copy(c_ref.at[piece], c_all.at[piece], c_sem.at[at])

    @pl.when(step_at == 0)
    def _():
        copies = load_table(parts, table, sem)
        for copy in copies:
            copy.start()
        for_each(steps, lambda at: block_copy(at).start())
        note_late(late_from, tid, live, late, late_count)
        for copy in copies:
            copy.wait()

    block_copy(step_at).wait()

    def step(i, carry):
        i0 = pl.multiple_of(i * GROUP, GROUP)
        n0 = first + i0
        base = pl.multiple_of(n0 * CHUNKS, GROUP * CHUNKS)
        for u in range(GROUP // 8):
            for c in range(0, CHUNKS, 2):
                x = c_all[pl.ds(base + (u * CHUNKS + c) * 8, 16), :].astype(f32)
                scr[pl.ds(u * 8 * PITCH + c, 8, stride=PITCH), :] = x[:8]
                scr[pl.ds(u * 8 * PITCH + c + 1, 8, stride=PITCH), :] = x[8:]
        for n in range(GROUP):
            c = scr[n * PITCH:n * PITCH + H, :].astype(bf16)
            t = tid[n0 + n]
            product = left_product(table[jnp.minimum(t, late_from - 1)], c, low).astype(bf16)
            o_ref[i0 + n] = jnp.where(t < late_from, product, c)
        return carry

    @pl.when(first < live[0])
    def _():
        lax.fori_loop(0, block // GROUP, step, 0, unroll=8)


def left(coupling, tid, live, parts, late_from):
    slots = coupling.shape[0]
    block = 128
    entries = sum(p.shape[0] for p in parts)
    return pl.pallas_call(
        functools.partial(left_kernel, len(parts), block, late_from),
        grid_spec=pltpu.PrefetchScalarGridSpec(
            num_scalar_prefetch=2,
            grid=(slots // block,),
            in_specs=[IN_HBM] + [ANYWHERE] * len(parts),
            out_specs=[pl.BlockSpec((block, H, LANES), lambda g, *_: (g, 0, 0)), SCALARS, SCALARS],
            scratch_shapes=[
                pltpu.VMEM((entries, H, LANES), bf16),
                pltpu.VMEM((slots * CHUNKS, LANES), bf16),
                pltpu.VMEM((GROUP * PITCH + SPARE, LANES), f32),
                pltpu.SemaphoreType.DMA((len(parts),)),
                pltpu.SemaphoreType.DMA((slots // block,)),
            ],
        ),
        out_shape=[
            jax.ShapeDtypeStruct((slots, H, LANES), bf16),
            jax.ShapeDtypeStruct((slots + LATE_GROUP,), jnp.int32),
            jax.ShapeDtypeStruct((1,), jnp.int32),
        ],
        compiler_params=pltpu.CompilerParams(vmem_limit_bytes=44 * 2**20),
        cost_estimate=pl.CostEstimate(
            flops=8 * coupling.size * W, bytes_accessed=8 * coupling.size, transcendentals=0
        ),
    )(tid, live, slot_rows(coupling), *parts)


def right_kernel(
    n_late, n_parts, chips, block, late_from, tid, sid, live, late, late_count, chip, left_ref, *refs
):
    late_parts, parts = refs[:n_late], refs[n_late:n_late + n_parts]
    o_ref, left_all, late_table, table, out_all, scr = refs[n_late + n_parts:-4]
    sem, late_sem, l_sem, o_sem = refs[-4:]
    low = low_lanes()
    slots = tid.shape[0]
    rows = block * CHUNKS
    blocks = (live[0] + block - 1) // block

    def left_copy(at):
        piece = pl.ds(pl.multiple_of(at * block, block), block)
        return pltpu.make_async_copy(left_ref.at[piece], left_all.at[piece], l_sem.at[at])

    def out_copy(at):
        piece = pl.ds(pl.multiple_of(at * rows, rows), rows)
        return pltpu.make_async_copy(out_all.at[piece], o_ref.at[piece], o_sem.at[at])

    def here(at):
        far = at // 2 + 2 - chips
        there = jnp.where(chip[0] % 2 == 0, chip[0] + far, chip[0] - far)
        return (there >= 0) & (there < chips)

    last = load_table(late_parts, late_table, late_sem)
    columns = load_table(parts, table, sem)
    for copy in last:
        copy.start()
    for_each(blocks, lambda at: left_copy(at).start())
    for at, copy in enumerate(columns):
        pl.when(here(at))(copy.start)

    def clear(at):
        at = blocks + at
        out_all[pl.ds(pl.multiple_of(at * rows, rows), rows), :] = jnp.zeros((rows, LANES), bf16)
        out_copy(at).start()

    for_each(slots // block - blocks, clear)
    for copy in last:
        copy.wait()
    for_each(blocks, lambda at: left_copy(at).wait())

    if n_late:
        def fill(i):
            which = [late[i * LATE_GROUP + n] for n in range(LATE_GROUP)]
            held = [left_all[w] for w in which]
            done = []
            for w, c in zip(which, held):
                t = jnp.maximum(tid[jnp.minimum(w, slots - 1)] - late_from, 0)
                done.append(left_product(late_table[t], c, low).astype(bf16))
            for w, product in zip(which, done):
                left_all[w] = product

        for_each((late_count[0] + LATE_GROUP - 1) // LATE_GROUP, fill)
    for at, copy in enumerate(columns):
        pl.when(here(at))(copy.wait)

    def step(i, carry):
        n0 = pl.multiple_of(i * GROUP, GROUP)
        for n in range(GROUP):
            scr[n * PITCH:n * PITCH + H, :] = right_product(left_all[n0 + n], table[sid[n0 + n]], low)
        keep = lax.broadcasted_iota(jnp.int32, (8, LANES), 0) + n0
        base = pl.multiple_of(n0 * CHUNKS, GROUP * CHUNKS)
        for u in range(GROUP // 8):
            mask = keep + u * 8 < live[0]
            for c in range(0, CHUNKS, 2):
                pair = [
                    jnp.where(mask, scr[pl.ds(u * 8 * PITCH + c + e, 8, stride=PITCH), :], 0.0)
                    for e in range(2)
                ]
                out_all[pl.ds(base + (u * CHUNKS + c) * 8, 16), :] = jnp.concatenate(pair, axis=0).astype(bf16)
        return carry

    per = block // GROUP

    def work(at):
        lax.fori_loop(0, per, lambda i, carry: step(at * per + i, carry), 0, unroll=12)
        out_copy(at).start()

    for_each(blocks, work)
    for_each(slots // block, lambda at: out_copy(at).wait())


def right(left_all, tid, sid, live, late, late_count, chip, late_parts, parts, late_from, chips):
    slots = left_all.shape[0]
    block = 192 if slots % 128 == 0 else GROUP
    n_late, entries = sum(p.shape[0] for p in late_parts), sum(p.shape[0] for p in parts)
    rows = pl.pallas_call(
        functools.partial(right_kernel, len(late_parts), len(parts), chips, block, late_from),
        in_specs=[SCALARS] * 6 + [ANYWHERE] * (1 + len(late_parts) + len(parts)),
        out_specs=ANYWHERE,
        scratch_shapes=[
            pltpu.VMEM((slots + 1, H, LANES), bf16),
            pltpu.VMEM((max(n_late, 8), H, LANES), bf16),
            pltpu.VMEM((entries, H, LANES), bf16),
            pltpu.VMEM((slots * CHUNKS, LANES), bf16),
            pltpu.VMEM((GROUP * PITCH + SPARE, LANES), f32),
            pltpu.SemaphoreType.DMA((len(parts),)),
            pltpu.SemaphoreType.DMA((max(len(late_parts), 1),)),
            pltpu.SemaphoreType.DMA((slots // block,)),
            pltpu.SemaphoreType.DMA((slots // block,)),
        ],
        out_shape=jax.ShapeDtypeStruct((slots * CHUNKS, LANES), bf16),
        compiler_params=pltpu.CompilerParams(vmem_limit_bytes=30 * 2**20),
    )(tid, sid, live, late, late_count, chip, left_all, *late_parts, *parts)
    return slot_rows_back(rows)


def square_pairs(rows):
    near, far = [], []
    for row in range(rows):
        for at in range(4):
            near.append((row * 4 + at, row * 4 + (at ^ (1 + row % 2))))
            far.append((row * 4 + at, row * 4 + (at ^ (2 - row % 2))))
    return near, far


def pass_on(part, pairs):
    return lax.ppermute(part, ("tgt", "src"), pairs)


def column_pairs(chips):
    def far(z):
        return z if z in (0, chips - 1) else ((z - 1) ^ 1) + 1

    near_pairs = [(2 * z + c, 2 * (z ^ 1) + c) for z in range(chips) for c in range(2)]
    far_pairs = [(2 * z + c, 2 * far(z) + c) for z in range(chips) for c in range(2)]
    return near_pairs, far_pairs, [(i, i ^ 1) for i in range(2 * chips)]


def send(part, pairs):
    return lax.ppermute(part, "tgt", pairs)


def slot_tables(n_src, chips, row, col, t_shape, s_shape, block_tgt, block_src, block_cone):
    t_clu, t_cones = t_shape
    s_clu, s_cones = s_shape
    tloc = jnp.clip(block_tgt - row * t_clu, 0, t_clu - 1)
    sloc = jnp.clip(block_src - col * s_clu, 0, s_clu - 1)
    owner = block_cone // t_cones
    if n_src == 4:
        part = owner ^ col
        part = jnp.where((part % 3 != 0) & (row % 2 == 1), 3 - part, part)
        tid = (part * t_clu + tloc) * t_cones + block_cone % t_cones
        late_from = 3 * t_clu * t_cones
    else:
        tid = (owner * t_clu + tloc) * t_cones + block_cone % t_cones
        late_from = n_src * t_clu * t_cones
    owner = block_cone // s_cones
    z = row // 2
    ahead = (owner // 2 - z) * (1 - 2 * (z % 2))
    part = (ahead + chips - 2) * 2 + ((owner ^ row) & 1)
    return tid, late_from, (part * s_clu + sloc) * s_cones + block_cone % s_cones


def local(n_src, chips, tgt_weight, src_weight, coupling, block_tgt, block_src, block_cone, block_count, tgt_transfer):
    row, col = lax.axis_index("tgt"), lax.axis_index("src")
    near, far, cores = column_pairs(chips)
    fence = lax.optimization_barrier
    square = n_src == 4
    t_shape, s_shape = tgt_weight.shape[:2], src_weight.shape[:2]

    s_dense = prep_src(src_weight)
    a, b = send(s_dense, near), send(s_dense, far)
    t_dense = prep_tgt(tgt_weight)
    kept, t_dense = fence((s_dense, t_dense))
    own = [s_dense, send(kept, cores)]
    slots = (block_tgt, block_src, block_cone)
    a, b, own, tgt_transfer, slots = fence((a, b, own, tgt_transfer, slots))
    if square:
        one, other = square_pairs(2 * chips)
        p, q = pass_on(t_dense, one), pass_on(t_dense, other)
    else:
        gathered = lax.all_gather(t_dense, "src", axis=0).reshape(-1, H, LANES)

    tid, late_from, sid = slot_tables(n_src, chips, row, col, t_shape, s_shape, *slots)
    new_transfer = transfer(t_dense, tgt_transfer)
    ahead_parts, behind_parts = [], []
    for step in range(2, chips):
        kept_a = a
        kept_b, new_transfer = fence((b, new_transfer)) if step == 2 else (b, new_transfer)
        a, b = send(b, near), send(a, far) if step < chips - 1 else None
        if step == 3 and square:
            kept_a, kept_b = kept_x, kept_y
        ahead_parts.append([kept_a, send(kept_a, cores)])
        behind_parts.append([kept_b, send(kept_b, cores)])
        if step == 2 and square:
            a, b, new_transfer = fence((a, b, new_transfer))
            p, q, tid, sid, kept_x, kept_y, ahead_parts = fence((p, q, tid, sid, a, b, ahead_parts))
            d = pass_on(p, other)

    t_parts, late_parts = ([t_dense, p, q], [d]) if square else ([gathered], [])
    left_all, late, late_count = left(coupling, tid, block_count, t_parts, late_from)
    a, left_all = fence((a, left_all))
    ahead_parts.append([a, send(a, cores)])
    s_parts = sum(behind_parts[::-1] + [own] + ahead_parts, [])
    chip = (row // 2).reshape(1)
    new_coupling = right(
        left_all, tid, sid, block_count, late, late_count, chip, late_parts, s_parts, late_from, chips
    )
    return new_coupling, new_transfer


def solution(mesh):
    n_src, chips = mesh.shape["src"], mesh.shape["tgt"] // 2
    both = ("tgt", "src")
    return jax.shard_map(
        functools.partial(local, n_src, chips),
        mesh=mesh,
        in_specs=(
            P("tgt", "src", None),
            P("src", "tgt", None),
            P(both, None),
            P(both),
            P(both),
            P(both),
            P(both),
            P("tgt", "src", None),
        ),
        out_specs=(P(both, None), P("tgt", "src", None)),
        check_vma=False,
    )
```

```python
import functools

import jax
import jax.numpy as jnp
from jax import lax
from jax.experimental import pallas as pl
from jax.experimental.pallas import tpu as pltpu
from jax.sharding import PartitionSpec as P

W = 64
WW = 4096
CONES = 16
H = W // 2
LANES = 2 * W
CHUNKS = WW // LANES
SPARE = 2 * H
PITCH = H + 1
GROUP = 16
f32, bf16 = jnp.float32, jnp.bfloat16
LATE_GROUP = 64
SMALL, LARGE = 12 * 2**20, 60 * 2**20


def swap_halves(x):
    return jnp.concatenate([x[:, W:], x[:, :W]], axis=1)


def low_lanes():
    return lax.broadcasted_iota(jnp.int32, (H, LANES), 1) < W


def left_product(t, c, low):
    lhs = jnp.concatenate([t[:, :W], t[:, W:]], axis=0)
    rhs = jnp.concatenate([c, swap_halves(c)], axis=0)
    y = jnp.dot(lhs, rhs, preferred_element_type=f32)
    return jnp.where(low, y[:H], y[H:])


def right_product(left, s, low):
    lhs = jnp.concatenate([left[:, :W], left[:, W:]], axis=0).astype(bf16)
    turned = swap_halves(s)
    rhs = jnp.concatenate([jnp.where(low, s, turned), jnp.where(low, turned, s)], axis=0)
    y = jnp.dot(lhs, rhs, preferred_element_type=f32)
    return jnp.where(low, y[:H], y[H:])


def rows_of(array):
    n, cones, _ = array.shape
    return array.reshape(n, cones, CHUNKS, LANES).transpose(0, 2, 1, 3).reshape(n, CHUNKS * cones, LANES)


def rows_back(rows, cones):
    n = rows.shape[0]
    return rows.reshape(n, CHUNKS, cones, LANES).transpose(0, 2, 1, 3).reshape(n, cones, WW)


def slot_rows(array):
    n = array.shape[0]
    return array.reshape(n // 8, 8, CHUNKS, LANES).transpose(0, 2, 1, 3).reshape(n * CHUNKS, LANES)


def slot_rows_back(rows):
    n = rows.shape[0] // CHUNKS
    return rows.reshape(n // 8, CHUNKS, 8, LANES).transpose(0, 2, 1, 3).reshape(n, WW)


def every(start, count, pitch):
    return pl.ds(start, count) if pitch == 1 else pl.ds(start, count, stride=pitch)


WHOLE = pl.BlockSpec(memory_space=pltpu.VMEM)
ANYWHERE = pl.BlockSpec(memory_space=pl.ANY)
IN_HBM = pl.BlockSpec(memory_space=pltpu.HBM)
SCALARS = pl.BlockSpec(memory_space=pltpu.SMEM)


def prep_src_kernel(cones, s_ref, s_out, scr):
    row = lax.broadcasted_iota(jnp.int32, (LANES, 4 * LANES), 0)
    lane = lax.broadcasted_iota(jnp.int32, (LANES, 4 * LANES), 1)
    same = (row // H) == (lane // LANES)
    even = jnp.where(same & (lane % W == 2 * (row % H)), 1.0, 0.0).astype(bf16)
    odd = jnp.where(same & (lane % W == 2 * (row % H) + 1), 1.0, 0.0).astype(bf16)
    low = low_lanes()
    rows = CHUNKS * cones
    clusters = 8 // cones

    def turn(i, carry):
        for u in range(clusters):
            scr[u * rows:(u + 1) * rows, :] = s_ref[i * clusters + u].astype(f32)
        blocks = [scr[every(u * rows + k, H, cones), :] for u in range(clusters) for k in range(cones)]
        for half in range(2):
            up = jnp.concatenate(blocks[4 * half:4 * half + 4], axis=0).T.astype(bf16)
            both = jnp.dot(up[:W], even, preferred_element_type=f32) + jnp.dot(
                up[W:], odd, preferred_element_type=f32
            )
            for m in range(4):
                d = both[:, m * LANES:(m + 1) * LANES]
                s_out[i * 8 + 4 * half + m] = jnp.where(low, d[:H], d[H:]).astype(bf16)
        return carry

    lax.fori_loop(0, s_out.shape[0] // 8, turn, 0, unroll=4)


def prep_src(src_weight):
    n, cones = src_weight.shape[0], src_weight.shape[1]
    return pl.pallas_call(
        functools.partial(prep_src_kernel, cones),
        in_specs=[WHOLE],
        out_specs=WHOLE,
        out_shape=jax.ShapeDtypeStruct((n * cones, H, LANES), bf16),
        scratch_shapes=[pltpu.VMEM((8 * H + SPARE, LANES), f32)],
        compiler_params=pltpu.CompilerParams(vmem_limit_bytes=SMALL),
    )(rows_of(src_weight))


def prep_tgt_kernel(cones, t_ref, out, scr):
    row = lax.broadcasted_iota(jnp.int32, (LANES, LANES), 0)
    lane = lax.broadcasted_iota(jnp.int32, (LANES, LANES), 1)
    g, at = lane // W, lane % W
    odd_col = (at // H) ^ g
    order = jnp.where(row == g * W + 2 * (at % H) + odd_col, 1.0, 0.0).astype(bf16)
    rows = CHUNKS * cones

    def sort(i, carry):
        for u in range(2):
            at = 2 * i + u
            scr[u * rows:(u + 1) * rows, :] = jnp.dot(t_ref[at], order, preferred_element_type=f32)
            for k in range(cones):
                out[at * cones + k] = scr[every(u * rows + k, H, cones), :].astype(bf16)
        return carry

    lax.fori_loop(0, t_ref.shape[0] // 2, sort, 0, unroll=4)


def prep_tgt(tgt_weight):
    n, cones = tgt_weight.shape[0], tgt_weight.shape[1]
    return pl.pallas_call(
        functools.partial(prep_tgt_kernel, cones),
        in_specs=[WHOLE],
        out_specs=WHOLE,
        out_shape=jax.ShapeDtypeStruct((n * cones, H, LANES), bf16),
        scratch_shapes=[pltpu.VMEM((2 * CHUNKS * cones + SPARE, LANES), f32)],
        compiler_params=pltpu.CompilerParams(vmem_limit_bytes=SMALL),
    )(rows_of(tgt_weight))


def transfer_kernel(cones, t_ref, x_ref, o_ref, x_scr, o_scr):
    low = low_lanes()
    rows = CHUNKS * cones

    def one(i, carry):
        for u in range(2):
            at = 2 * i + u
            x_scr[u * rows:(u + 1) * rows, :] = x_ref[at].astype(f32)
            for k in range(cones):
                x = x_scr[every(u * rows + k, H, cones), :].astype(bf16)
                o_scr[every(u * rows + k, H, cones), :] = left_product(t_ref[at * cones + k], x, low)
            o_ref[at] = o_scr[u * rows:(u + 1) * rows, :].astype(bf16)
        return carry

    lax.fori_loop(0, x_ref.shape[0] // 2, one, 0, unroll=2)


def transfer(t_dense, tgt_transfer):
    cones = tgt_transfer.shape[1]
    rows = rows_of(tgt_transfer)
    out = pl.pallas_call(
        functools.partial(transfer_kernel, cones),
        in_specs=[WHOLE, WHOLE],
        out_specs=WHOLE,
        out_shape=jax.ShapeDtypeStruct(rows.shape, bf16),
        scratch_shapes=[pltpu.VMEM((2 * CHUNKS * cones + SPARE, LANES), f32)] * 2,
        compiler_params=pltpu.CompilerParams(vmem_limit_bytes=24 * 2**20),
        cost_estimate=pl.CostEstimate(flops=2 * rows.size * W, bytes_accessed=12 * rows.size, transcendentals=0),
    )(t_dense, rows)
    return rows_back(out, cones)


def load_table(parts, table, sem):
    copies, at = [], 0
    for part in parts:
        copies.append(pltpu.make_async_copy(part, table.at[pl.ds(at, part.shape[0])], sem.at[len(copies)]))
        at += part.shape[0]
    return copies


def for_each(count, act):
    def one(at, carry):
        act(at)
        return carry

    lax.fori_loop(0, count, one, 0)


def note_late(late_from, tid, live, late, late_count):
    slots = tid.shape[0]

    def note(n, count):
        late[count] = n
        return count + jnp.where((tid[n] >= late_from) & (n < live[0]), 1, 0)

    count = lax.fori_loop(0, slots, note, 0, unroll=8)
    late_count[0] = count

    def pad(n, carry):
        late[count + n] = slots
        return carry

    lax.fori_loop(0, LATE_GROUP, pad, 0)


def left_kernel(n_parts, block, late_from, tid, live, c_ref, *refs):
    parts = refs[:n_parts]
    o_ref, late, late_count, table, c_all, scr, sem, c_sem = refs[n_parts:]
    step_at, steps = pl.program_id(0), pl.num_programs(0)
    first = step_at * block
    low = low_lanes()
    rows = block * CHUNKS

    def block_copy(at):
        piece = pl.ds(pl.multiple_of(at * rows, rows), rows)
        return pltpu.make_async_copy(c_ref.at[piece], c_all.at[piece], c_sem.at[at])

    @pl.when(step_at == 0)
    def _():
        copies = load_table(parts, table, sem)
        for copy in copies:
            copy.start()
        for_each(steps, lambda at: block_copy(at).start())
        note_late(late_from, tid, live, late, late_count)
        for copy in copies:
            copy.wait()

    block_copy(step_at).wait()

    def step(i, carry):
        i0 = pl.multiple_of(i * GROUP, GROUP)
        n0 = first + i0
        base = pl.multiple_of(n0 * CHUNKS, GROUP * CHUNKS)
        for u in range(GROUP // 8):
            for c in range(0, CHUNKS, 2):
                x = c_all[pl.ds(base + (u * CHUNKS + c) * 8, 16), :].astype(f32)
                scr[pl.ds(u * 8 * PITCH + c, 8, stride=PITCH), :] = x[:8]
                scr[pl.ds(u * 8 * PITCH + c + 1, 8, stride=PITCH), :] = x[8:]
        for n in range(GROUP):
            c = scr[n * PITCH:n * PITCH + H, :].astype(bf16)
            t = tid[n0 + n]
            product = left_product(table[jnp.minimum(t, late_from - 1)], c, low).astype(bf16)
            o_ref[i0 + n] = jnp.where(t < late_from, product, c)
        return carry

    @pl.when(first < live[0])
    def _():
        lax.fori_loop(0, block // GROUP, step, 0, unroll=8)


def left(coupling, tid, live, parts, late_from):
    slots = coupling.shape[0]
    block = 128
    entries = sum(p.shape[0] for p in parts)
    return pl.pallas_call(
        functools.partial(left_kernel, len(parts), block, late_from),
        grid_spec=pltpu.PrefetchScalarGridSpec(
            num_scalar_prefetch=2,
            grid=(slots // block,),
            in_specs=[IN_HBM] + [ANYWHERE] * len(parts),
            out_specs=[pl.BlockSpec((block, H, LANES), lambda g, *_: (g, 0, 0)), SCALARS, SCALARS],
            scratch_shapes=[
                pltpu.VMEM((entries, H, LANES), bf16),
                pltpu.VMEM((slots * CHUNKS, LANES), bf16),
                pltpu.VMEM((GROUP * PITCH + SPARE, LANES), f32),
                pltpu.SemaphoreType.DMA((len(parts),)),
                pltpu.SemaphoreType.DMA((slots // block,)),
            ],
        ),
        out_shape=[
            jax.ShapeDtypeStruct((slots, H, LANES), bf16),
            jax.ShapeDtypeStruct((slots + LATE_GROUP,), jnp.int32),
            jax.ShapeDtypeStruct((1,), jnp.int32),
        ],
        compiler_params=pltpu.CompilerParams(vmem_limit_bytes=44 * 2**20),
        cost_estimate=pl.CostEstimate(
            flops=8 * coupling.size * W, bytes_accessed=8 * coupling.size, transcendentals=0
        ),
    )(tid, live, slot_rows(coupling), *parts)


def right_kernel(
    n_late, n_parts, chips, block, late_from, tid, sid, live, late, late_count, chip, left_ref, *refs
):
    late_parts, parts = refs[:n_late], refs[n_late:n_late + n_parts]
    o_ref, left_all, late_table, table, out_all, scr = refs[n_late + n_parts:-4]
    sem, late_sem, l_sem, o_sem = refs[-4:]
    low = low_lanes()
    slots = tid.shape[0]
    rows = block * CHUNKS
    blocks = (live[0] + block - 1) // block

    def left_copy(at):
        piece = pl.ds(pl.multiple_of(at * block, block), block)
        return pltpu.make_async_copy(left_ref.at[piece], left_all.at[piece], l_sem.at[at])

    def out_copy(at):
        piece = pl.ds(pl.multiple_of(at * rows, rows), rows)
        return pltpu.make_async_copy(out_all.at[piece], o_ref.at[piece], o_sem.at[at])

    def here(at):
        far = at // 2 + 2 - chips
        there = jnp.where(chip[0] % 2 == 0, chip[0] + far, chip[0] - far)
        return (there >= 0) & (there < chips)

    last = load_table(late_parts, late_table, late_sem)
    columns = load_table(parts, table, sem)
    for copy in last:
        copy.start()
    for_each(blocks, lambda at: left_copy(at).start())
    for at, copy in enumerate(columns):
        pl.when(here(at))(copy.start)

    def clear(at):
        at = blocks + at
        out_all[pl.ds(pl.multiple_of(at * rows, rows), rows), :] = jnp.zeros((rows, LANES), bf16)
        out_copy(at).start()

    for_each(slots // block - blocks, clear)
    for copy in last:
        copy.wait()
    for_each(blocks, lambda at: left_copy(at).wait())

    if n_late:
        def fill(i):
            which = [late[i * LATE_GROUP + n] for n in range(LATE_GROUP)]
            held = [left_all[w] for w in which]
            done = []
            for w, c in zip(which, held):
                t = jnp.maximum(tid[jnp.minimum(w, slots - 1)] - late_from, 0)
                done.append(left_product(late_table[t], c, low).astype(bf16))
            for w, product in zip(which, done):
                left_all[w] = product

        for_each((late_count[0] + LATE_GROUP - 1) // LATE_GROUP, fill)
    for at, copy in enumerate(columns):
        pl.when(here(at))(copy.wait)

    def step(i, carry):
        n0 = pl.multiple_of(i * GROUP, GROUP)
        for n in range(GROUP):
            scr[n * PITCH:n * PITCH + H, :] = right_product(left_all[n0 + n], table[sid[n0 + n]], low)
        keep = lax.broadcasted_iota(jnp.int32, (8, LANES), 0) + n0
        base = pl.multiple_of(n0 * CHUNKS, GROUP * CHUNKS)
        for u in range(GROUP // 8):
            mask = keep + u * 8 < live[0]
            for c in range(0, CHUNKS, 2):
                pair = [
                    jnp.where(mask, scr[pl.ds(u * 8 * PITCH + c + e, 8, stride=PITCH), :], 0.0)
                    for e in range(2)
                ]
                out_all[pl.ds(base + (u * CHUNKS + c) * 8, 16), :] = jnp.concatenate(pair, axis=0).astype(bf16)
        return carry

    per = block // GROUP

    def work(at):
        lax.fori_loop(0, per, lambda i, carry: step(at * per + i, carry), 0, unroll=12)
        out_copy(at).start()

    for_each(blocks, work)
    for_each(slots // block, lambda at: out_copy(at).wait())


def right(left_all, tid, sid, live, late, late_count, chip, late_parts, parts, late_from, chips):
    slots = left_all.shape[0]
    block = 192 if slots % 128 == 0 else GROUP
    n_late, entries = sum(p.shape[0] for p in late_parts), sum(p.shape[0] for p in parts)
    rows = pl.pallas_call(
        functools.partial(right_kernel, len(late_parts), len(parts), chips, block, late_from),
        in_specs=[SCALARS] * 6 + [ANYWHERE] * (1 + len(late_parts) + len(parts)),
        out_specs=ANYWHERE,
        scratch_shapes=[
            pltpu.VMEM((slots + 1, H, LANES), bf16),
            pltpu.VMEM((max(n_late, 8), H, LANES), bf16),
            pltpu.VMEM((entries, H, LANES), bf16),
            pltpu.VMEM((slots * CHUNKS, LANES), bf16),
            pltpu.VMEM((GROUP * PITCH + SPARE, LANES), f32),
            pltpu.SemaphoreType.DMA((len(parts),)),
            pltpu.SemaphoreType.DMA((max(len(late_parts), 1),)),
            pltpu.SemaphoreType.DMA((slots // block,)),
            pltpu.SemaphoreType.DMA((slots // block,)),
        ],
        out_shape=jax.ShapeDtypeStruct((slots * CHUNKS, LANES), bf16),
        compiler_params=pltpu.CompilerParams(vmem_limit_bytes=30 * 2**20),
    )(tid, sid, live, late, late_count, chip, left_all, *late_parts, *parts)
    return slot_rows_back(rows)


def square_pairs(rows):
    near, far = [], []
    for row in range(rows):
        for at in range(4):
            near.append((row * 4 + at, row * 4 + (at ^ (1 + row % 2))))
            far.append((row * 4 + at, row * 4 + (at ^ (2 - row % 2))))
    return near, far


def pass_on(part, pairs):
    return lax.ppermute(part, ("tgt", "src"), pairs)


def column_pairs(chips):
    def far(z):
        return z if z in (0, chips - 1) else ((z - 1) ^ 1) + 1

    near_pairs = [(2 * z + c, 2 * (z ^ 1) + c) for z in range(chips) for c in range(2)]
    far_pairs = [(2 * z + c, 2 * far(z) + c) for z in range(chips) for c in range(2)]
    return near_pairs, far_pairs, [(i, i ^ 1) for i in range(2 * chips)]


def send(part, pairs):
    return lax.ppermute(part, "tgt", pairs)


def slot_tables(n_src, chips, row, col, t_shape, s_shape, block_tgt, block_src, block_cone):
    t_clu, t_cones = t_shape
    s_clu, s_cones = s_shape
    tloc = jnp.clip(block_tgt - row * t_clu, 0, t_clu - 1)
    sloc = jnp.clip(block_src - col * s_clu, 0, s_clu - 1)
    owner = block_cone // t_cones
    if n_src == 4:
        part = owner ^ col
        part = jnp.where((part % 3 != 0) & (row % 2 == 1), 3 - part, part)
        tid = (part * t_clu + tloc) * t_cones + block_cone % t_cones
        late_from = 3 * t_clu * t_cones
    else:
        tid = (owner * t_clu + tloc) * t_cones + block_cone % t_cones
        late_from = n_src * t_clu * t_cones
    owner = block_cone // s_cones
    z = row // 2
    ahead = (owner // 2 - z) * (1 - 2 * (z % 2))
    part = (ahead + chips - 2) * 2 + ((owner ^ row) & 1)
    return tid, late_from, (part * s_clu + sloc) * s_cones + block_cone % s_cones


def local(n_src, chips, tgt_weight, src_weight, coupling, block_tgt, block_src, block_cone, block_count, tgt_transfer):
    row, col = lax.axis_index("tgt"), lax.axis_index("src")
    near, far, cores = column_pairs(chips)
    fence = lax.optimization_barrier
    square = n_src == 4
    t_shape, s_shape = tgt_weight.shape[:2], src_weight.shape[:2]

    s_dense = prep_src(src_weight)
    a, b = send(s_dense, near), send(s_dense, far)
    t_dense = prep_tgt(tgt_weight)
    kept, t_dense = fence((s_dense, t_dense))
    own = [s_dense, send(kept, cores)]
    slots = (block_tgt, block_src, block_cone)
    a, b, own, tgt_transfer, slots = fence((a, b, own, tgt_transfer, slots))
    if square:
        one, other = square_pairs(2 * chips)
        p, q = pass_on(t_dense, one), pass_on(t_dense, other)
    else:
        gathered = lax.all_gather(t_dense, "src", axis=0).reshape(-1, H, LANES)

    tid, late_from, sid = slot_tables(n_src, chips, row, col, t_shape, s_shape, *slots)
    new_transfer = transfer(t_dense, tgt_transfer)
    ahead_parts, behind_parts = [], []
    for step in range(2, chips):
        kept_a = a
        kept_b, new_transfer = fence((b, new_transfer)) if step == 2 else (b, new_transfer)
        a, b = send(b, near), send(a, far) if step < chips - 1 else None
        if step == 3 and square:
            kept_a, kept_b = kept_x, kept_y
        ahead_parts.append([kept_a, send(kept_a, cores)])
        behind_parts.append([kept_b, send(kept_b, cores)])
        if step == 2 and square:
            a, b, new_transfer = fence((a, b, new_transfer))
            p, q, tid, sid, kept_x, kept_y, ahead_parts = fence((p, q, tid, sid, a, b, ahead_parts))
            d = pass_on(p, other)

    t_parts, late_parts = ([t_dense, p, q], [d]) if square else ([gathered], [])
    left_all, late, late_count = left(coupling, tid, block_count, t_parts, late_from)
    a, left_all = fence((a, left_all))
    ahead_parts.append([a, send(a, cores)])
    s_parts = sum(behind_parts[::-1] + [own] + ahead_parts, [])
    chip = (row // 2).reshape(1)
    new_coupling = right(
        left_all, tid, sid, block_count, late, late_count, chip, late_parts, s_parts, late_from, chips
    )
    return new_coupling, new_transfer


def solution(mesh):
    n_src, chips = mesh.shape["src"], mesh.shape["tgt"] // 2
    both = ("tgt", "src")
    return jax.shard_map(
        functools.partial(local, n_src, chips),
        mesh=mesh,
        in_specs=(
            P("tgt", "src", None),
            P("src", "tgt", None),
            P(both, None),
            P(both),
            P(both),
            P(both),
            P(both),
            P("tgt", "src", None),
        ),
        out_specs=(P(both, None), P("tgt", "src", None)),
        check_vma=False,
    )
```
